256 devices in a mesh: sub: 16 (over x_hi, z), blk: 16 (over x_lo, y, core).
Axes of the slice: x: 4 (x_hi: 2, x_lo: 2; x = x_hi * 2 + x_lo), y: 4, z: 8, core: 2. Of those that a mesh axis runs over, the one named last changes fastest.
Arguments:
- coefficients: float32 [1024, 4, 2, 64, 128], P('sub', None, None, 'blk'), may hold values from -0.2 to 0.2
- owner_slot: int32 [1024], P('sub'), may hold values from 0 to 1023, as said below
- child_list: int32 [1024, 8], P('sub'), may hold values from 0 to 7, each once within a row
Outputs:
- children: float32 [1024, 4, 8, 64, 2, 128], P('sub', None, None, 'blk')
The draws below stay inside these ranges and needn't reach their ends.
Inputs may be any that keep to these rules, and one draw needn't show every extreme that they name: owner_slot is a permutation of the 1024 positions; position s belongs to subtree index s // 64; of the 64 boxes held by one subtree index exactly 4 belong to each subtree index. `child_list`: each row lists the 8 octant codes once each.
All inputs are finite; a program needn't handle non-finite values.
Results may differ from the reference program's by a relative error of at most 0.0003.
Values sent between devices are 32-bit elements; how exact they have to be, the bound alone decides.
No kernel may reach another device: no remote copies, remote signals or barrier semaphores. Data moves between devices by JAX's collectives and lax.ppermute only.
A program may use at most 64 MiB of HBM per device.

```python
import jax
import jax.numpy as jnp
from jax import lax

L = 64
M = 128
J = 64
K = 128
BOX_DEV = 64
NRHS = 4
BOXES = 1024


def draw_owner_slot(key, part):
    sub_count = BOXES // BOX_DEV
    per_peer = BOX_DEV // sub_count
    first_key, second_key = jax.random.split(jax.random.fold_in(key, 11), 2)
    local_order = jax.vmap(lambda one: jax.random.permutation(one, BOX_DEV))(jax.random.split(first_key, sub_count))
    inside = jax.vmap(lambda one: jax.random.permutation(one, BOX_DEV))(jax.random.split(second_key, sub_count))
    ranks = jnp.arange(BOX_DEV, dtype=jnp.int32)
    target = ranks // per_peer
    within = ranks % per_peer
    sources = jnp.arange(sub_count, dtype=jnp.int32)[:, None]
    positions = inside[target[None, :], sources * per_peer + within[None, :]]
    slot_by_rank = target[None, :] * BOX_DEV + positions
    inverse = jnp.argsort(local_order, axis=1)
    slots = jnp.take_along_axis(slot_by_rank, inverse, axis=1)
    return slots.reshape(BOXES).astype(jnp.int32)


def steps_of(own_key, shape, cuts, least, largest):
    loudness, own = 1.0, jax.random.fold_in(own_key, 6)
    for position, blocks in cuts:
        heights = jnp.exp(jax.random.uniform(jax.random.fold_in(own, position), (blocks,), jnp.float32, least / len(cuts), largest / len(cuts)))
        loudness = loudness * jnp.repeat(heights, shape[position] // blocks).reshape([-1 if axis == position else 1 for axis in range(len(shape))])
    return loudness


def centred(rng, extent, width, reach, cuts=(), kind=jnp.bfloat16):
    entries = width * jax.random.normal(rng, extent, jnp.float32)
    if cuts:
        entries = entries * steps_of(rng, extent, cuts, -0.22, 0.18)
    return jnp.clip(entries, -reach, reach).astype(kind)


def setup_inputs(seed: int = 0) -> dict:
    key_of = jax.random.split(jax.random.key(seed), 4)
    coefficients = centred(key_of[0], (BOXES, NRHS, 2, L, M), 0.03, 0.2, ((0, 16), (3, 16)), jnp.float32)
    owner_slot = draw_owner_slot(jax.random.fold_in(key_of[3], 71), 0)
    child_list = jax.vmap(lambda own: jax.random.permutation(own, 8))(jax.random.split(key_of[2], BOXES)).reshape((BOXES, 8)).astype(jnp.int32)
    return {"coefficients": coefficients, "owner_slot": owner_slot, "child_list": child_list}


def legendre_table(orders_abs, polar, degrees):
    cosines = jnp.cos(polar)[None, :]
    sines = jnp.sin(polar)[None, :]
    order_col = orders_abs[:, None]
    log_start = 0.5 * (jnp.log((2.0 * order_col + 1.0) / (4.0 * jnp.pi)) + lax.lgamma(2.0 * order_col + 1.0) - order_col * jnp.log(4.0) - 2.0 * lax.lgamma(order_col + 1.0)) + order_col * jnp.log(sines)
    diag_value = jnp.exp(log_start)
    next_value = jnp.sqrt(2.0 * order_col + 3.0) * cosines * diag_value

    def advance(state, degree):
        previous, before, factor_prev = state
        numer = jnp.maximum(4.0 * degree * degree - 1.0, 1.0)
        denom = jnp.maximum(degree * degree - order_col * order_col, 1.0)
        factor = jnp.sqrt(numer / denom)
        recur = factor * (cosines * previous - before / factor_prev)
        value = jnp.where(degree < order_col, 0.0, jnp.where(degree == order_col, diag_value, jnp.where(degree == order_col + 1.0, next_value, recur)))
        return ((value, previous, factor), value)
    zeros = jnp.zeros_like(diag_value)
    start_state = (zeros, zeros, jnp.ones_like(order_col))
    _, values = lax.scan(advance, start_state, jnp.arange(degrees).astype(jnp.float32))
    return values

def dft_table(degrees, columns, azimuths):
    column_ids = jnp.arange(columns, dtype=jnp.int32)
    azimuth_ids = jnp.arange(azimuths, dtype=jnp.int32)
    turns = jnp.mod((column_ids[:, None] - degrees) * azimuth_ids[None, :], azimuths)
    angle = 2.0 * jnp.pi * turns.astype(jnp.float32) / azimuths
    cosine = jnp.cos(angle)
    sine = jnp.sin(angle)
    upper = jnp.concatenate([cosine, sine], axis=1)
    lower = jnp.concatenate([-sine, cosine], axis=1)
    return jnp.concatenate([upper, lower], axis=0)

def shift_children(waves, octants, polar, azimuths):
    azimuth = 2.0 * jnp.pi * jnp.arange(azimuths).astype(jnp.float32) / azimuths
    dir_x = jnp.sin(polar)[:, None] * jnp.cos(azimuth)[None, :]
    dir_y = jnp.sin(polar)[:, None] * jnp.sin(azimuth)[None, :]
    dir_z = jnp.cos(polar)[:, None] * jnp.ones_like(azimuth)[None, :]
    sign_x = (2 * (octants & 1) - 1).astype(jnp.float32)[:, None, None]
    sign_y = (2 * (octants >> 1 & 1) - 1).astype(jnp.float32)[:, None, None]
    sign_z = (2 * (octants >> 2 & 1) - 1).astype(jnp.float32)[:, None, None]
    phase = 5.5 * (sign_x * dir_x[None] + sign_y * dir_y[None] + sign_z * dir_z[None])
    phase_cos = jnp.cos(phase)[None]
    phase_sin = jnp.sin(phase)[None]
    wave_re = waves[:, :, 0, :][:, None]
    wave_im = waves[:, :, 1, :][:, None]
    real_part = wave_re * phase_cos - wave_im * phase_sin
    imag_part = wave_re * phase_sin + wave_im * phase_cos
    return jnp.stack([real_part, imag_part], axis=-2)

def reference(coefficients, owner_slot, child_list):
    owned = coefficients[jnp.argsort(owner_slot)]
    polar = jnp.pi * (jnp.arange(J).astype(jnp.float32) + 0.5) / J
    orders_abs = jnp.abs(jnp.arange(M) - L).astype(jnp.float32)
    table = legendre_table(orders_abs, polar, L)
    spectral = dft_table(L, M, K)
    cases = coefficients.shape[1]

    def one_box(inputs):
        expansion, octants = inputs
        cycles = jnp.einsum('rxlc,lcj->rjxc', expansion, table, precision=lax.Precision.HIGHEST)
        waves = jnp.dot(cycles.reshape(cases * J, 2 * M), spectral, precision=lax.Precision.HIGHEST)
        return shift_children(waves.reshape(cases, J, 2, K), octants, polar, K)
    return lax.map(one_box, (owned, child_list))
```

```python
import math

import jax
import jax.numpy as jnp
import ml_dtypes
import numpy as np
from jax import lax
from jax.experimental import pallas as pl
from jax.experimental.pallas import tpu as pltpu
from jax.sharding import PartitionSpec as P

L = 64
M = 128
J = 64
K = 128
HALF = J // 2
F32 = jnp.float32
BF16 = jnp.bfloat16


def legendre_half():
    order = np.abs(np.arange(M) - L).astype(np.float64)[None, :]
    polar = (np.pi * (np.arange(HALF) + 0.5) / J)[:, None]
    cosines, sines = np.cos(polar), np.sin(polar)
    lgamma = np.vectorize(math.lgamma)
    start = np.exp(
        0.5 * (np.log((2 * order + 1) / (4 * np.pi)) + lgamma(2 * order + 1) - order * np.log(4.0) - 2 * lgamma(order + 1))
        + order * np.log(sines)
    )
    following = np.sqrt(2 * order + 3) * cosines * start
    previous = before = np.zeros_like(start)
    factor_before = np.ones_like(order)
    rows = []
    for degree in range(L):
        factor = np.sqrt(np.maximum(4.0 * degree * degree - 1, 1) / np.maximum(degree * degree - order * order, 1))
        recur = factor * (cosines * previous - before / factor_before)
        value = np.where(degree < order, 0.0, np.where(degree == order, start, np.where(degree == order + 1, following, recur)))
        rows.append(value)
        previous, before, factor_before = value, previous, factor
    return np.stack(rows).astype(np.float32)


def dft_halves():
    turns = ((np.arange(M)[:, None] - L) * np.arange(K)[None, :]) % K
    angle = 2 * np.pi * turns / K
    cosine, sine = np.cos(angle), np.sin(angle)
    full = np.block([[cosine, sine], [-sine, cosine]])
    high = full.astype(ml_dtypes.bfloat16)
    rest = (full - high.astype(np.float64)).astype(ml_dtypes.bfloat16)
    return high, rest


def shift_tables(blk_count):
    polar = np.pi * (np.arange(J) + 0.5) / J
    azimuth = 2 * np.pi * np.arange(K) / K
    octant = np.arange(8)
    sign = [(2 * ((octant >> bit) & 1) - 1)[:, None, None] for bit in range(3)]
    phase = 5.5 * (
        sign[0] * (np.sin(polar)[:, None] * np.cos(azimuth))[None]
        + sign[1] * (np.sin(polar)[:, None] * np.sin(azimuth))[None]
        + sign[2] * (np.cos(polar)[:, None] * np.ones(K))[None]
    )
    cosine = np.stack([np.cos(phase), np.cos(phase)], axis=2)
    sine = np.stack([-np.sin(phase), np.sin(phase)], axis=2)
    width = J // blk_count

    def cut(table):
        table = table.reshape(8, blk_count, width * 2, K)
        return np.ascontiguousarray(table.transpose(1, 0, 2, 3)).astype(np.float32)

    return cut(cosine), cut(sine)


def pack_kernel(sub_count, me_ref, slot_ref, coef_ref, out_ref, place_ref, count):
    box_count = coef_ref.shape[0]
    per_peer = box_count // sub_count
    for peer in range(sub_count):
        count[peer] = 0
    row = lax.broadcasted_iota(jnp.int32, place_ref.shape, 0)
    lane = lax.broadcasted_iota(jnp.int32, place_ref.shape, 1)
    first = me_ref[0] * per_peer
    place = jnp.zeros(place_ref.shape, jnp.int32)
    for box in range(box_count):
        slot = slot_ref[box]
        peer = slot // box_count
        rank = count[peer]
        count[peer] = rank + 1
        out_ref[peer * per_peer + rank] = coef_ref[box]
        here = (row == peer) & (lane == first + rank)
        place = jnp.where(here, slot - peer * box_count, place)
    place_ref[...] = place


def spread(value, order):
    return jnp.take_along_axis(value, order, axis=0)


def transform_kernel(blk_count, in_ref, table_ref, high_ref, rest_ref, out_ref, cycles):
    boxes = in_ref.shape[0] // blk_count
    degrees = L // blk_count
    group = 2
    vregs = HALF // 8
    lane = lax.broadcasted_iota(jnp.int32, (8, M), 1)
    mirror = jnp.where(lane % 2 == 0, 1.0, -1.0).astype(F32)

    def legendre(step, carry):
        sums = [[[None] * vregs for _ in range(2)] for _ in range(2 * group)]
        for degree in range(L):
            source, row = degree // degrees, degree % degrees
            table = [table_ref[degree, 8 * v : 8 * v + 8, :] for v in range(vregs)]
            for one in range(2 * group):
                box, part = step * group + one // 2, one % 2
                at = part * degrees + row
                value = in_ref[box * blk_count + source, at : at + 1, :]
                wide = jnp.broadcast_to(value, (8, M))
                for v in range(vregs):
                    term = wide * table[v]
                    old = sums[one][degree % 2][v]
                    sums[one][degree % 2][v] = term if old is None else old + term
        for one in range(2 * group):
            box, part = step * group + one // 2, one % 2
            for v in range(vregs):
                even, odd = sums[one][0][v], sums[one][1][v]
                low = pl.multiple_of(box * J + 8 * v, 8)
                high = pl.multiple_of(box * J + HALF + 8 * v, 8)
                cycles[pl.ds(low, 8), part * M : part * M + M] = even + odd
                cycles[pl.ds(high, 8), part * M : part * M + M] = (even - odd) * mirror
        return carry

    lax.fori_loop(0, boxes // group, legendre, 0)

    width = J // blk_count
    sub_row = lax.broadcasted_iota(jnp.int32, (8, K), 0)
    real_row = sub_row % 2 == 0
    step_row = sub_row // 2
    chunk = 4

    def azimuths(step, carry):
        base = pl.multiple_of(step * (chunk * J), chunk * J)
        left = cycles[pl.ds(base, chunk * J), :]
        left_high = left.astype(BF16)
        left_rest = (left - left_high.astype(F32)).astype(BF16)
        waves = jnp.dot(left_high, high_ref[...], preferred_element_type=F32)
        waves += jnp.dot(left_rest, high_ref[...], preferred_element_type=F32)
        waves += jnp.dot(left_high, rest_ref[...], preferred_element_type=F32)
        for one in range(chunk):
            for blk in range(blk_count):
                first = blk * width
                if first < HALF:
                    at, order = first // 8 * 8, first % 8 + step_row
                else:
                    low = J - 1 - first
                    at, order = HALF + low // 8 * 8, low % 8 - step_row
                start = one * J + at
                real = spread(waves[start : start + 8, :K], order)
                imag = spread(waves[start : start + 8, K:], order)
                out_ref[blk, step * chunk + one] = jnp.where(real_row, real, imag)
        return carry

    lax.fori_loop(0, boxes // chunk, azimuths, 0)


def shift_kernel(boxes, sub_count, me_ref, place_ref, child_ref, in_ref, cos_ref, sin_ref, out_ref, inverse):
    per_peer = boxes // sub_count
    cases = 4

    @pl.when(pl.program_id(0) == 0)
    def _():
        for arrival in range(boxes):
            inverse[place_ref[arrival]] = arrival

    even = lax.broadcasted_iota(jnp.int32, (8, K), 0) % 2 == 0
    count = out_ref.shape[0]

    def one_box(at, carry):
        box = pl.program_id(0) * count + at
        arrival = inverse[box]
        source = arrival // per_peer
        rank = arrival % per_peer
        waves = [in_ref[rank * cases + case, source] for case in range(cases)]
        crossed = [jnp.where(even, pltpu.roll(w, 7, 0), pltpu.roll(w, 1, 0)) for w in waves]
        for child in range(8):
            octant = child_ref[box, child]
            cosine, sine = cos_ref[0, octant], sin_ref[0, octant]
            for case in range(cases):
                out_ref[at, case * 8 + child] = waves[case] * cosine + crossed[case] * sine
        return carry

    lax.fori_loop(0, count, one_box, 0)


def body(coefficients, owner_slot, child_list):
    box_count, cases = coefficients.shape[:2]
    sub_count = lax.axis_size("sub")
    blk_count = lax.axis_size("blk")
    per_peer = box_count // sub_count
    vmem = pl.BlockSpec(memory_space=pltpu.VMEM)
    smem = pl.BlockSpec(memory_space=pltpu.SMEM)
    sub_index = lax.axis_index("sub").reshape(1)
    blk_index = lax.axis_index("blk").reshape(1)

    outgoing, places = pl.pallas_call(
        lambda *refs: pack_kernel(sub_count, *refs),
        out_shape=(
            jax.ShapeDtypeStruct((box_count, cases * 8, M), F32),
            jax.ShapeDtypeStruct((sub_count, box_count), jnp.int32),
        ),
        in_specs=[smem, smem, vmem],
        out_specs=(vmem, vmem),
        scratch_shapes=[pltpu.SMEM((sub_count,), jnp.int32)],
        name="pack",
    )(sub_index, owner_slot, coefficients.reshape(box_count, cases * 8, M))
    arrived_places = lax.psum_scatter(places, "sub", scatter_dimension=0, tiled=False)

    arrived = lax.all_to_all(outgoing.reshape(box_count * cases, 8, M), ("sub", "blk"), 0, 0, tiled=True)

    high, rest = dft_halves()
    waves = pl.pallas_call(
        lambda *refs: transform_kernel(blk_count, *refs),
        out_shape=jax.ShapeDtypeStruct((blk_count, sub_count, 8, K), F32),
        in_specs=[vmem] * 4,
        out_specs=vmem,
        scratch_shapes=[pltpu.VMEM((sub_count * J, 2 * M), F32)],
        name="transform",
    )(arrived, jnp.asarray(legendre_half()), jnp.asarray(high), jnp.asarray(rest))

    rows = lax.all_to_all(waves, "blk", 0, 0, tiled=True)

    cosine, sine = shift_tables(blk_count)
    step = 4
    children = pl.pallas_call(
        lambda *refs: shift_kernel(box_count, sub_count, *refs),
        out_shape=jax.ShapeDtypeStruct((box_count, cases * 8, 8, K), F32),
        grid_spec=pltpu.PrefetchScalarGridSpec(
            num_scalar_prefetch=3,
            grid=(box_count // step,),
            in_specs=[
                vmem,
                pl.BlockSpec((1, 8, 8, K), lambda i, me, place, child: (me[0], 0, 0, 0)),
                pl.BlockSpec((1, 8, 8, K), lambda i, me, place, child: (me[0], 0, 0, 0)),
            ],
            out_specs=pl.BlockSpec((step, cases * 8, 8, K), lambda i, me, place, child: (i, 0, 0, 0)),
            scratch_shapes=[pltpu.SMEM((box_count,), jnp.int32)],
        ),
        name="shift",
    )(blk_index, arrived_places, child_list, rows, jnp.asarray(cosine), jnp.asarray(sine))
    return children.reshape(box_count, cases, 8, J // blk_count, 2, K)


def solution(mesh):
    placed = (P("sub", None, None, "blk", None), P("sub"), P("sub", None))
    return jax.shard_map(
        body,
        mesh=mesh,
        in_specs=placed,
        out_specs=P("sub", None, None, "blk", None, None),
        check_vma=False,
    )
```

```python
import math

import jax
import jax.numpy as jnp
import ml_dtypes
import numpy as np
from jax import lax
from jax.experimental import pallas as pl
from jax.experimental.pallas import tpu as pltpu
from jax.sharding import PartitionSpec as P

L = 64
M = 128
J = 64
K = 128
HALF = J // 2
F32 = jnp.float32
BF16 = jnp.bfloat16


def legendre_half():
    order = np.abs(np.arange(M) - L).astype(np.float64)[None, :]
    polar = (np.pi * (np.arange(HALF) + 0.5) / J)[:, None]
    cosines, sines = np.cos(polar), np.sin(polar)
    lgamma = np.vectorize(math.lgamma)
    start = np.exp(
        0.5 * (np.log((2 * order + 1) / (4 * np.pi)) + lgamma(2 * order + 1) - order * np.log(4.0) - 2 * lgamma(order + 1))
        + order * np.log(sines)
    )
    following = np.sqrt(2 * order + 3) * cosines * start
    previous = before = np.zeros_like(start)
    factor_before = np.ones_like(order)
    rows = []
    for degree in range(L):
        factor = np.sqrt(np.maximum(4.0 * degree * degree - 1, 1) / np.maximum(degree * degree - order * order, 1))
        recur = factor * (cosines * previous - before / factor_before)
        value = np.where(degree < order, 0.0, np.where(degree == order, start, np.where(degree == order + 1, following, recur)))
        rows.append(value)
        previous, before, factor_before = value, previous, factor
    return np.stack(rows).astype(np.float32)


def dft_halves():
    turns = ((np.arange(M)[:, None] - L) * np.arange(K)[None, :]) % K
    angle = 2 * np.pi * turns / K
    cosine, sine = np.cos(angle), np.sin(angle)
    full = np.block([[cosine, sine], [-sine, cosine]])
    high = full.astype(ml_dtypes.bfloat16)
    rest = (full - high.astype(np.float64)).astype(ml_dtypes.bfloat16)
    return high, rest


def shift_tables(blk_count):
    polar = np.pi * (np.arange(J) + 0.5) / J
    azimuth = 2 * np.pi * np.arange(K) / K
    octant = np.arange(8)
    sign = [(2 * ((octant >> bit) & 1) - 1)[:, None, None] for bit in range(3)]
    phase = 5.5 * (
        sign[0] * (np.sin(polar)[:, None] * np.cos(azimuth))[None]
        + sign[1] * (np.sin(polar)[:, None] * np.sin(azimuth))[None]
        + sign[2] * (np.cos(polar)[:, None] * np.ones(K))[None]
    )
    cosine = np.stack([np.cos(phase), np.cos(phase)], axis=2)
    sine = np.stack([-np.sin(phase), np.sin(phase)], axis=2)
    width = J // blk_count

    def cut(table):
        table = table.reshape(8, blk_count, width * 2, K)
        return np.ascontiguousarray(table.transpose(1, 0, 2, 3)).astype(np.float32)

    return cut(cosine), cut(sine)


def pack_kernel(sub_count, me_ref, slot_ref, coef_ref, out_ref, place_ref, count, moved):
    box_count = coef_ref.shape[0]
    per_peer = box_count // sub_count
    for peer in range(sub_count):
        count[peer] = 0
    row = lax.broadcasted_iota(jnp.int32, place_ref.shape, 0)
    lane = lax.broadcasted_iota(jnp.int32, place_ref.shape, 1)
    first = me_ref[0] * per_peer
    place = jnp.zeros(place_ref.shape, jnp.int32)
    for box in range(box_count):
        slot = slot_ref[box]
        peer = slot // box_count
        rank = count[peer]
        count[peer] = rank + 1
        pltpu.make_async_copy(coef_ref.at[box], out_ref.at[peer * per_peer + rank], moved).start()
        here = (row == peer) & (lane == first + rank)
        place = jnp.where(here, slot - peer * box_count, place)
    place_ref[...] = place
    pltpu.make_async_copy(coef_ref, out_ref, moved).wait()


def spread(value, order):
    return jnp.take_along_axis(value, order, axis=0)


def transform_kernel(
    blk_count, in_ref, table_hbm, high_hbm, rest_hbm, place_ref, out_ref,
    table_ref, high_ref, rest_ref, cycles, made, table_in, dft_in, moved,
):
    del place_ref
    pieces = table_in.shape[0]
    cut = L // pieces
    arriving = []
    for piece in range(pieces):
        part = pl.ds(piece * cut, cut)
        arriving.append(pltpu.make_async_copy(table_hbm.at[part], table_ref.at[part], table_in.at[piece]))
    dft = [
        pltpu.make_async_copy(high_hbm, high_ref, dft_in.at[0]),
        pltpu.make_async_copy(rest_hbm, rest_ref, dft_in.at[1]),
    ]
    for copy in arriving + dft:
        copy.start()
    boxes = in_ref.shape[0] // blk_count
    degrees = L // blk_count
    group = 2
    vregs = HALF // 8
    lane = lax.broadcasted_iota(jnp.int32, (8, M), 1)
    mirror = jnp.where(lane % 2 == 0, 1.0, -1.0).astype(F32)

    def legendre(step, slot, first=False):
        sums = [[[None] * vregs for _ in range(2)] for _ in range(2 * group)]
        for degree in range(L):
            source, row = degree // degrees, degree % degrees
            if first and degree % cut == 0:
                arriving[degree // cut].wait()
            table = [table_ref[degree, 8 * v : 8 * v + 8, :] for v in range(vregs)]
            for one in range(2 * group):
                box, part = step * group + one // 2, one % 2
                at = part * degrees + row
                value = in_ref[box * blk_count + source, at : at + 1, :]
                wide = jnp.broadcast_to(value, (8, M))
                for v in range(vregs):
                    term = wide * table[v]
                    old = sums[one][degree % 2][v]
                    sums[one][degree % 2][v] = term if old is None else old + term
        for one in range(2 * group):
            box, part = one // 2, one % 2
            for v in range(vregs):
                even, odd = sums[one][0][v], sums[one][1][v]
                low, high = box * J + 8 * v, box * J + HALF + 8 * v
                cycles[slot, low : low + 8, part * M : part * M + M] = even + odd
                cycles[slot, high : high + 8, part * M : part * M + M] = (even - odd) * mirror

    width = J // blk_count
    sub_row = lax.broadcasted_iota(jnp.int32, (8, K), 0)
    real_row = sub_row % 2 == 0
    step_row = sub_row // 2

    def azimuths(step, slot):
        left = cycles[slot]
        left_high = left.astype(BF16)
        left_rest = (left - left_high.astype(F32)).astype(BF16)
        waves = jnp.dot(left_high, high_ref[...], preferred_element_type=F32)
        waves += jnp.dot(left_rest, high_ref[...], preferred_element_type=F32)
        waves += jnp.dot(left_high, rest_ref[...], preferred_element_type=F32)
        for one in range(group):
            for blk in range(blk_count):
                first = blk * width
                if first < HALF:
                    at, order = first // 8 * 8, first % 8 + step_row
                else:
                    low = J - 1 - first
                    at, order = HALF + low // 8 * 8, low % 8 - step_row
                start = one * J + at
                real = spread(waves[start : start + 8, :K], order)
                imag = spread(waves[start : start + 8, K:], order)
                made[blk, step * group + one] = jnp.where(real_row, real, imag)
        part = pl.ds(step * group, group)
        pltpu.make_async_copy(made.at[:, part], out_ref.at[:, part], moved).start()

    steps = boxes // group
    legendre(0, 0, first=True)
    for copy in dft:
        copy.wait()

    def both(step, carry):
        azimuths(step - 1, (step - 1) % 2)
        legendre(step, step % 2)
        return carry

    lax.fori_loop(1, steps, both, 0)
    azimuths(steps - 1, (steps - 1) % 2)
    pltpu.make_async_copy(made, out_ref, moved).wait()


def shift_kernel(boxes, sub_count, me_ref, place_ref, child_ref, in_ref, turn_ref, out_ref, made, moved):
    per_peer = boxes // sub_count
    cases = 4
    even = lax.broadcasted_iota(jnp.int32, (8, K), 0) % 2 == 0
    me = me_ref[0]

    def one_box(arrival, carry):
        box = place_ref[me, arrival]
        source = arrival // per_peer
        rank = arrival % per_peer
        waves = [in_ref[rank * cases + case, source] for case in range(cases)]
        crossed = [jnp.where(even, pltpu.roll(w, 7, 0), pltpu.roll(w, 1, 0)) for w in waves]
        for child in range(8):
            octant = child_ref[box, child]
            cosine, sine = turn_ref[octant, 0], turn_ref[octant, 1]
            for case in range(cases):
                made[arrival, case * 8 + child] = waves[case] * cosine + crossed[case] * sine
        pltpu.make_async_copy(made.at[arrival], out_ref.at[box], moved).start()
        return carry

    lax.fori_loop(0, boxes, one_box, 0, unroll=2)
    pltpu.make_async_copy(made, out_ref, moved).wait()


def body(coefficients, owner_slot, child_list):
    box_count, cases = coefficients.shape[:2]
    sub_count = lax.axis_size("sub")
    blk_count = lax.axis_size("blk")
    vmem = pl.BlockSpec(memory_space=pltpu.VMEM)
    smem = pl.BlockSpec(memory_space=pltpu.SMEM)
    anywhere = pl.BlockSpec(memory_space=pl.ANY)
    near = lambda array: pltpu.with_memory_space_constraint(array, pltpu.VMEM)
    far = lambda array: pltpu.with_memory_space_constraint(array, pltpu.HBM)
    sub_index = lax.axis_index("sub").reshape(1)
    limit = pltpu.CompilerParams(vmem_limit_bytes=16 * 2**20)

    outgoing, places = pl.pallas_call(
        lambda *refs: pack_kernel(sub_count, *refs),
        out_shape=(
            jax.ShapeDtypeStruct((box_count, cases * 8, M), F32),
            jax.ShapeDtypeStruct((sub_count, box_count), jnp.int32),
        ),
        in_specs=[smem, smem, anywhere],
        out_specs=(anywhere, vmem),
        scratch_shapes=[pltpu.SMEM((sub_count,), jnp.int32), pltpu.SemaphoreType.DMA],
        compiler_params=limit,
        name="pack",
    )(sub_index, far(owner_slot), far(coefficients.reshape(box_count, cases * 8, M)))
    places = lax.psum(places, "sub")

    arrived = lax.all_to_all(outgoing.reshape(box_count * cases, 8, M), ("sub", "blk"), 0, 0, tiled=True)

    high, rest = dft_halves()
    waves = pl.pallas_call(
        lambda *refs: transform_kernel(blk_count, *refs),
        out_shape=jax.ShapeDtypeStruct((blk_count, sub_count, 8, K), F32),
        in_specs=[vmem] + [anywhere] * 4,
        out_specs=anywhere,
        scratch_shapes=[
            pltpu.VMEM((L, HALF, M), F32),
            pltpu.VMEM((2 * M, 2 * K), BF16),
            pltpu.VMEM((2 * M, 2 * K), BF16),
            pltpu.VMEM((2, 2 * J, 2 * M), F32),
            pltpu.VMEM((blk_count, sub_count, 8, K), F32),
            pltpu.SemaphoreType.DMA((4,)),
            pltpu.SemaphoreType.DMA((2,)),
            pltpu.SemaphoreType.DMA,
        ],
        compiler_params=limit,
        name="transform",
    )(near(arrived), far(jnp.asarray(legendre_half())), far(jnp.asarray(high)), far(jnp.asarray(rest)), places)

    rows = lax.all_to_all(waves, "blk", 0, 0, tiled=True)

    turns = jnp.asarray(np.stack(shift_tables(blk_count), axis=2))
    turns = lax.dynamic_index_in_dim(turns, lax.axis_index("blk"), 0, keepdims=False)
    children = pl.pallas_call(
        lambda *refs: shift_kernel(box_count, sub_count, *refs),
        out_shape=jax.ShapeDtypeStruct((box_count, cases * 8, 8, K), F32),
        in_specs=[smem, smem, smem, vmem, vmem],
        out_specs=anywhere,
        scratch_shapes=[pltpu.VMEM((box_count, cases * 8, 8, K), F32), pltpu.SemaphoreType.DMA],
        compiler_params=limit,
        name="shift",
    )(sub_index, places, child_list, near(rows), near(turns))
    return children.reshape(box_count, cases, 8, J // blk_count, 2, K)


def solution(mesh):
    placed = (P("sub", None, None, "blk", None), P("sub"), P("sub", None))
    return jax.shard_map(
        body,
        mesh=mesh,
        in_specs=placed,
        out_specs=P("sub", None, None, "blk", None, None),
        check_vma=False,
    )
```

```python
import math

import jax
import jax.numpy as jnp
import ml_dtypes
import numpy as np
from jax import lax
from jax.experimental import pallas as pl
from jax.experimental.pallas import tpu as pltpu
from jax.sharding import PartitionSpec as P

L = 64
M = 128
J = 64
K = 128
HALF = J // 2
F32 = jnp.float32
BF16 = jnp.bfloat16


def legendre_half():
    order = np.abs(np.arange(M) - L).astype(np.float64)[None, :]
    polar = (np.pi * (np.arange(HALF) + 0.5) / J)[:, None]
    cosines, sines = np.cos(polar), np.sin(polar)
    lgamma = np.vectorize(math.lgamma)
    start = np.exp(
        0.5 * (np.log((2 * order + 1) / (4 * np.pi)) + lgamma(2 * order + 1) - order * np.log(4.0) - 2 * lgamma(order + 1))
        + order * np.log(sines)
    )
    following = np.sqrt(2 * order + 3) * cosines * start
    previous = before = np.zeros_like(start)
    factor_before = np.ones_like(order)
    rows = []
    for degree in range(L):
        factor = np.sqrt(np.maximum(4.0 * degree * degree - 1, 1) / np.maximum(degree * degree - order * order, 1))
        recur = factor * (cosines * previous - before / factor_before)
        value = np.where(degree < order, 0.0, np.where(degree == order, start, np.where(degree == order + 1, following, recur)))
        rows.append(value)
        previous, before, factor_before = value, previous, factor
    return np.stack(rows).astype(np.float32)


def dft_halves():
    turns = ((np.arange(M)[:, None] - L) * np.arange(K)[None, :]) % K
    angle = 2 * np.pi * turns / K
    cosine, sine = np.cos(angle), np.sin(angle)
    full = np.block([[cosine, sine], [-sine, cosine]])
    high = full.astype(ml_dtypes.bfloat16)
    rest = (full - high.astype(np.float64)).astype(ml_dtypes.bfloat16)
    return high, rest


def shift_tables(blk_count):
    polar = np.pi * (np.arange(J) + 0.5) / J
    azimuth = 2 * np.pi * np.arange(K) / K
    octant = np.arange(8)
    sign = [(2 * ((octant >> bit) & 1) - 1)[:, None, None] for bit in range(3)]
    phase = 5.5 * (
        sign[0] * (np.sin(polar)[:, None] * np.cos(azimuth))[None]
        + sign[1] * (np.sin(polar)[:, None] * np.sin(azimuth))[None]
        + sign[2] * (np.cos(polar)[:, None] * np.ones(K))[None]
    )
    cosine = np.stack([np.cos(phase), np.cos(phase)], axis=2)
    sine = np.stack([-np.sin(phase), np.sin(phase)], axis=2)
    width = J // blk_count

    def cut(table):
        table = table.reshape(8, blk_count, width * 2, K)
        return np.ascontiguousarray(table.transpose(1, 0, 2, 3)).astype(np.float32)

    return cut(cosine), cut(sine)


def pack_kernel(sub_count, me_ref, slot_ref, coef_ref, out_ref, place_ref, held, count, arrived, moved):
    box_count = coef_ref.shape[0]
    pieces = arrived.shape[0]
    cut = box_count // pieces
    arriving = []
    for piece in range(pieces):
        part = pl.ds(piece * cut, cut)
        arriving.append(pltpu.make_async_copy(coef_ref.at[part], held.at[part], arrived.at[piece]))
    for copy in arriving:
        copy.start()
    per_peer = box_count // sub_count
    for peer in range(sub_count):
        count[peer] = 0
    row = lax.broadcasted_iota(jnp.int32, place_ref.shape, 0)
    lane = lax.broadcasted_iota(jnp.int32, place_ref.shape, 1)
    first = me_ref[0] * per_peer
    place = jnp.zeros(place_ref.shape, jnp.int32)
    for box in range(box_count):
        if box % cut == 0:
            arriving[box // cut].wait()
        slot = slot_ref[box]
        peer = slot // box_count
        rank = count[peer]
        count[peer] = rank + 1
        pltpu.make_async_copy(held.at[box], out_ref.at[peer * per_peer + rank], moved).start()
        here = (row == peer) & (lane == first + rank)
        place = jnp.where(here, slot - peer * box_count, place)
    place_ref[...] = place
    pltpu.make_async_copy(held, out_ref, moved).wait()


def spread(value, order):
    return jnp.take_along_axis(value, order, axis=0)


def transform_kernel(
    blk_count, in_ref, table_hbm, high_hbm, rest_hbm, out_ref,
    table_ref, high_ref, rest_ref, cycles, made, table_in, dft_in, moved,
):
    pieces = table_in.shape[0]
    cut = L // pieces
    arriving = []
    for piece in range(pieces):
        part = pl.ds(piece * cut, cut)
        arriving.append(pltpu.make_async_copy(table_hbm.at[part], table_ref.at[part], table_in.at[piece]))
    dft = [
        pltpu.make_async_copy(high_hbm, high_ref, dft_in.at[0]),
        pltpu.make_async_copy(rest_hbm, rest_ref, dft_in.at[1]),
    ]
    for copy in arriving + dft:
        copy.start()
    boxes = in_ref.shape[0] // blk_count
    degrees = L // blk_count
    group = 2
    vregs = HALF // 8
    lane = lax.broadcasted_iota(jnp.int32, (8, M), 1)
    mirror = jnp.where(lane % 2 == 0, 1.0, -1.0).astype(F32)

    def legendre(step, slot, first=False):
        sums = [[[None] * vregs for _ in range(2)] for _ in range(2 * group)]
        for degree in range(L):
            source, row = degree // degrees, degree % degrees
            if first and degree % cut == 0:
                arriving[degree // cut].wait()
            table = [table_ref[degree, 8 * v : 8 * v + 8, :] for v in range(vregs)]
            for one in range(2 * group):
                box, part = step * group + one // 2, one % 2
                at = part * degrees + row
                value = in_ref[box * blk_count + source, at : at + 1, :]
                wide = jnp.broadcast_to(value, (8, M))
                for v in range(vregs):
                    term = wide * table[v]
                    old = sums[one][degree % 2][v]
                    sums[one][degree % 2][v] = term if old is None else old + term
        for one in range(2 * group):
            box, part = one // 2, one % 2
            for v in range(vregs):
                even, odd = sums[one][0][v], sums[one][1][v]
                low, high = box * J + 8 * v, box * J + HALF + 8 * v
                cycles[slot, low : low + 8, part * M : part * M + M] = even + odd
                cycles[slot, high : high + 8, part * M : part * M + M] = (even - odd) * mirror

    width = J // blk_count
    sub_row = lax.broadcasted_iota(jnp.int32, (8, K), 0)
    real_row = sub_row % 2 == 0
    step_row = sub_row // 2

    def azimuths(step, slot):
        left = cycles[slot]
        left_high = left.astype(BF16)
        left_rest = (left - left_high.astype(F32)).astype(BF16)
        waves = jnp.dot(left_high, high_ref[...], preferred_element_type=F32)
        waves += jnp.dot(left_rest, high_ref[...], preferred_element_type=F32)
        waves += jnp.dot(left_high, rest_ref[...], preferred_element_type=F32)
        for one in range(group):
            for blk in range(blk_count):
                first = blk * width
                if first < HALF:
                    at, order = first // 8 * 8, first % 8 + step_row
                else:
                    low = J - 1 - first
                    at, order = HALF + low // 8 * 8, low % 8 - step_row
                start = one * J + at
                real = spread(waves[start : start + 8, :K], order)
                imag = spread(waves[start : start + 8, K:], order)
                made[blk, step * group + one] = jnp.where(real_row, real, imag)
        part = pl.ds(step * group, group)
        pltpu.make_async_copy(made.at[:, part], out_ref.at[:, part], moved).start()

    steps = boxes // group
    legendre(0, 0, first=True)
    for copy in dft:
        copy.wait()

    def both(step, carry):
        azimuths(step - 1, (step - 1) % 2)
        legendre(step, step % 2)
        return carry

    lax.fori_loop(1, steps, both, 0)
    azimuths(steps - 1, (steps - 1) % 2)
    pltpu.make_async_copy(made, out_ref, moved).wait()


def shift_kernel(boxes, sub_count, me_ref, place_ref, child_ref, in_ref, turn_ref, out_ref, made, moved):
    per_peer = boxes // sub_count
    cases = 4
    even = lax.broadcasted_iota(jnp.int32, (8, K), 0) % 2 == 0
    me = me_ref[0]

    def one_box(arrival, carry):
        box = place_ref[me, arrival]
        source = arrival // per_peer
        rank = arrival % per_peer
        waves = [in_ref[rank * cases + case, source] for case in range(cases)]
        crossed = [jnp.where(even, pltpu.roll(w, 7, 0), pltpu.roll(w, 1, 0)) for w in waves]
        for child in range(8):
            octant = child_ref[box, child]
            cosine, sine = turn_ref[octant, 0], turn_ref[octant, 1]
            for case in range(cases):
                made[arrival, case * 8 + child] = waves[case] * cosine + crossed[case] * sine
        pltpu.make_async_copy(made.at[arrival], out_ref.at[box], moved).start()
        return carry

    lax.fori_loop(0, boxes, one_box, 0, unroll=2)
    pltpu.make_async_copy(made, out_ref, moved).wait()


def whole(space):
    return pl.BlockSpec(memory_space=space)


def limit(mebibytes):
    return pltpu.CompilerParams(vmem_limit_bytes=mebibytes * 2**20)


def near(array):
    return pltpu.with_memory_space_constraint(array, pltpu.VMEM)


def far(array):
    return pltpu.with_memory_space_constraint(array, pltpu.HBM)


def pack(sub_index, owner_slot, coefficients, sub_count):
    box_count = coefficients.shape[0]
    shape = (box_count, coefficients.size // (box_count * M), M)
    return pl.pallas_call(
        lambda *refs: pack_kernel(sub_count, *refs),
        out_shape=(
            jax.ShapeDtypeStruct(shape, F32),
            jax.ShapeDtypeStruct((sub_count, box_count), jnp.int32),
        ),
        in_specs=[whole(pltpu.SMEM), whole(pltpu.SMEM), whole(pl.ANY)],
        out_specs=(whole(pl.ANY), whole(pltpu.VMEM)),
        scratch_shapes=[
            pltpu.VMEM(shape, F32),
            pltpu.SMEM((sub_count,), jnp.int32),
            pltpu.SemaphoreType.DMA((4,)),
            pltpu.SemaphoreType.DMA,
        ],
        compiler_params=limit(16),
        name="pack",
    )(sub_index, far(owner_slot), far(coefficients.reshape(shape)))


def transform(arrived, blk_count):
    boxes = arrived.shape[0] // blk_count
    high, rest = dft_halves()
    made = (blk_count, boxes, 8, K)
    return pl.pallas_call(
        lambda *refs: transform_kernel(blk_count, *refs),
        out_shape=jax.ShapeDtypeStruct(made, F32),
        in_specs=[whole(pltpu.VMEM)] + [whole(pl.ANY)] * 3,
        out_specs=whole(pl.ANY),
        scratch_shapes=[
            pltpu.VMEM((L, HALF, M), F32),
            pltpu.VMEM((2 * M, 2 * K), BF16),
            pltpu.VMEM((2 * M, 2 * K), BF16),
            pltpu.VMEM((2, 2 * J, 2 * M), F32),
            pltpu.VMEM(made, F32),
            pltpu.SemaphoreType.DMA((4,)),
            pltpu.SemaphoreType.DMA((2,)),
            pltpu.SemaphoreType.DMA,
        ],
        compiler_params=limit(16),
        name="transform",
    )(near(arrived), far(jnp.asarray(legendre_half())), far(jnp.asarray(high)), far(jnp.asarray(rest)))


def shift(sub_index, places, child_list, rows, turns):
    sub_count, boxes = places.shape
    cases = rows.shape[0] * sub_count // boxes
    shape = (boxes, cases * 8, 8, K)
    return pl.pallas_call(
        lambda *refs: shift_kernel(boxes, sub_count, *refs),
        out_shape=jax.ShapeDtypeStruct(shape, F32),
        in_specs=[whole(pltpu.SMEM)] * 3 + [whole(pltpu.VMEM)] * 2,
        out_specs=whole(pl.ANY),
        scratch_shapes=[pltpu.VMEM(shape, F32), pltpu.SemaphoreType.DMA],
        compiler_params=limit(16),
        name="shift",
    )(sub_index, places, child_list, near(rows), near(turns))


def body(coefficients, owner_slot, child_list):
    box_count, cases = coefficients.shape[:2]
    blk_count = lax.axis_size("blk")
    sub_index = lax.axis_index("sub").reshape(1)

    outgoing, places = pack(sub_index, owner_slot, coefficients, lax.axis_size("sub"))
    arrived = lax.all_to_all(outgoing.reshape(box_count * cases, 8, M), ("sub", "blk"), 0, 0, tiled=True)
    waves = transform(arrived, blk_count)
    rows = lax.all_to_all(waves, "blk", 0, 0, tiled=True)
    places = lax.psum(places, "sub")
    turns = jnp.asarray(np.stack(shift_tables(blk_count), axis=2))
    turns = lax.dynamic_index_in_dim(turns, lax.axis_index("blk"), 0, keepdims=False)
    children = shift(sub_index, places, child_list, rows, turns)
    return children.reshape(box_count, cases, 8, J // blk_count, 2, K)


def solution(mesh):
    placed = (P("sub", None, None, "blk", None), P("sub"), P("sub", None))
    return jax.shard_map(
        body,
        mesh=mesh,
        in_specs=placed,
        out_specs=P("sub", None, None, "blk", None, None),
        check_vma=False,
    )
```

```python
import math

import jax
import jax.numpy as jnp
import ml_dtypes
import numpy as np
from jax import lax
from jax.experimental import pallas as pl
from jax.experimental.pallas import tpu as pltpu
from jax.sharding import PartitionSpec as P

L = 64
M = 128
J = 64
K = 128
HALF = J // 2
F32 = jnp.float32
BF16 = jnp.bfloat16


def legendre_half():
    order = np.abs(np.arange(M) - L).astype(np.float64)[None, :]
    polar = (np.pi * (np.arange(HALF) + 0.5) / J)[:, None]
    cosines, sines = np.cos(polar), np.sin(polar)
    lgamma = np.vectorize(math.lgamma)
    start = np.exp(
        0.5 * (np.log((2 * order + 1) / (4 * np.pi)) + lgamma(2 * order + 1) - order * np.log(4.0) - 2 * lgamma(order + 1))
        + order * np.log(sines)
    )
    following = np.sqrt(2 * order + 3) * cosines * start
    previous = before = np.zeros_like(start)
    factor_before = np.ones_like(order)
    rows = []
    for degree in range(L):
        factor = np.sqrt(np.maximum(4.0 * degree * degree - 1, 1) / np.maximum(degree * degree - order * order, 1))
        recur = factor * (cosines * previous - before / factor_before)
        value = np.where(degree < order, 0.0, np.where(degree == order, start, np.where(degree == order + 1, following, recur)))
        rows.append(value)
        previous, before, factor_before = value, previous, factor
    return np.stack(rows).astype(np.float32)


def dft_halves():
    turns = ((np.arange(M)[:, None] - L) * np.arange(K)[None, :]) % K
    angle = 2 * np.pi * turns / K
    cosine, sine = np.cos(angle), np.sin(angle)
    full = np.block([[cosine, sine], [-sine, cosine]])
    high = full.astype(ml_dtypes.bfloat16)
    rest = (full - high.astype(np.float64)).astype(ml_dtypes.bfloat16)
    return high, rest


def shift_tables(blk_count):
    polar = np.pi * (np.arange(J) + 0.5) / J
    azimuth = 2 * np.pi * np.arange(K) / K
    octant = np.arange(8)
    sign = [(2 * ((octant >> bit) & 1) - 1)[:, None, None] for bit in range(3)]
    phase = 5.5 * (
        sign[0] * (np.sin(polar)[:, None] * np.cos(azimuth))[None]
        + sign[1] * (np.sin(polar)[:, None] * np.sin(azimuth))[None]
        + sign[2] * (np.cos(polar)[:, None] * np.ones(K))[None]
    )
    cosine = np.stack([np.cos(phase), np.cos(phase)], axis=2)
    sine = np.stack([-np.sin(phase), np.sin(phase)], axis=2)
    width = J // blk_count

    def cut(table):
        table = table.reshape(8, blk_count, width * 2, K)
        return np.ascontiguousarray(table.transpose(1, 0, 2, 3)).astype(np.float32)

    return cut(cosine), cut(sine)


def pack_kernel(sub_count, slot_hbm, coef_hbm, out_ref, place_ref, slot_ref, held, slot_in, coef_in):
    box_count = coef_hbm.shape[0]
    per_peer = box_count // sub_count
    pieces = coef_in.shape[0]
    cut = box_count // pieces
    slots = pltpu.make_async_copy(slot_hbm, slot_ref, slot_in)
    slots.start()
    arriving = []
    for piece in range(pieces):
        part = pl.ds(piece * cut, cut)
        arriving.append(pltpu.make_async_copy(coef_hbm.at[part], held.at[part], coef_in.at[piece]))
    for copy in arriving:
        copy.start()
    row = lax.broadcasted_iota(jnp.int32, place_ref.shape, 0)
    lane = lax.broadcasted_iota(jnp.int32, place_ref.shape, 1)
    key = row * box_count + lane - lax.axis_index("sub") * per_peer
    place = jnp.zeros(place_ref.shape, jnp.int32)
    half = sub_count // 2
    counts = [jnp.int32(0), jnp.int32(0)]
    ranks = []
    slots.wait()
    for box in range(box_count):
        slot = slot_ref[box]
        peer = slot // box_count
        second = peer >= half
        shift_by = (peer % half) * 4
        word = jnp.where(second, counts[1], counts[0])
        rank = (word >> shift_by) & 7
        word = word + (jnp.int32(1) << shift_by)
        counts = [jnp.where(second, counts[0], word), jnp.where(second, word, counts[1])]
        place = jnp.where(key == peer * box_count + rank, slot % box_count, place)
        ranks.append(peer * per_peer + rank)
    place_ref[...] = place
    for box in range(box_count):
        if box % cut == 0:
            arriving[box // cut].wait()
        out_ref[ranks[box]] = held[box]


def stage_kernel(table_hbm, high_hbm, rest_hbm, turn_hbm, place_ref, table_ref, high_ref, rest_ref, turn_ref, moved):
    del place_ref
    pairs = [
        (table_hbm, table_ref),
        (high_hbm, high_ref),
        (rest_hbm, rest_ref),
        (turn_hbm.at[lax.axis_index("blk")], turn_ref),
    ]
    copies = [pltpu.make_async_copy(source, target, moved.at[at]) for at, (source, target) in enumerate(pairs)]
    for copy in copies:
        copy.start()
    for copy in copies:
        copy.wait()


def spread(value, order):
    return jnp.take_along_axis(value, order, axis=0)


def transform_kernel(blk_count, in_ref, table_ref, high_ref, rest_ref, out_ref, cycles, made, moved):
    boxes = in_ref.shape[0] // blk_count
    degrees = L // blk_count
    group = 2
    vregs = HALF // 8
    lane = lax.broadcasted_iota(jnp.int32, (8, M), 1)
    mirror = jnp.where(lane % 2 == 0, 1.0, -1.0).astype(F32)

    def legendre(step, slot):
        sums = [[[None] * vregs for _ in range(2)] for _ in range(2 * group)]
        for degree in range(L):
            source, row = degree // degrees, degree % degrees
            table = [table_ref[degree, 8 * v : 8 * v + 8, :] for v in range(vregs)]
            for one in range(2 * group):
                box, part = step * group + one // 2, one % 2
                at = part * degrees + row
                value = in_ref[box * blk_count + source, at : at + 1, :]
                wide = jnp.broadcast_to(value, (8, M))
                for v in range(vregs):
                    term = wide * table[v]
                    old = sums[one][degree % 2][v]
                    sums[one][degree % 2][v] = term if old is None else old + term
        for one in range(2 * group):
            box, part = one // 2, one % 2
            for v in range(vregs):
                even, odd = sums[one][0][v], sums[one][1][v]
                low, high = box * J + 8 * v, box * J + HALF + 8 * v
                cycles[slot, low : low + 8, part * M : part * M + M] = even + odd
                cycles[slot, high : high + 8, part * M : part * M + M] = (even - odd) * mirror

    width = J // blk_count
    sub_row = lax.broadcasted_iota(jnp.int32, (8, K), 0)
    real_row = sub_row % 2 == 0
    step_row = sub_row // 2

    def azimuths(step, slot):
        left = cycles[slot]
        left_high = left.astype(BF16)
        left_rest = (left - left_high.astype(F32)).astype(BF16)
        waves = jnp.dot(left_high, high_ref[...], preferred_element_type=F32)
        waves += jnp.dot(left_rest, high_ref[...], preferred_element_type=F32)
        waves += jnp.dot(left_high, rest_ref[...], preferred_element_type=F32)
        for one in range(group):
            for blk in range(blk_count):
                first = blk * width
                if first < HALF:
                    at, order = first // 8 * 8, first % 8 + step_row
                else:
                    low = J - 1 - first
                    at, order = HALF + low // 8 * 8, low % 8 - step_row
                start = one * J + at
                real = spread(waves[start : start + 8, :K], order)
                imag = spread(waves[start : start + 8, K:], order)
                made[blk, step * group + one] = jnp.where(real_row, real, imag)
        part = pl.ds(step * group, group)
        pltpu.make_async_copy(made.at[:, part], out_ref.at[:, part], moved).start()

    steps = boxes // group
    legendre(0, 0)
    for step in range(1, steps):
        azimuths(step - 1, (step - 1) % 2)
        legendre(step, step % 2)
    azimuths(steps - 1, (steps - 1) % 2)
    pltpu.make_async_copy(made, out_ref, moved).wait()


def shift_kernel(boxes, sub_count, place_ref, child_ref, in_ref, turn_ref, out_ref, made, moved):
    per_peer = boxes // sub_count
    cases = 4
    even = lax.broadcasted_iota(jnp.int32, (8, K), 0) % 2 == 0
    me = lax.axis_index("sub")

    def one_box(arrival, carry):
        box = place_ref[me, arrival]
        source = arrival // per_peer
        rank = arrival % per_peer
        waves = [in_ref[rank * cases + case, source] for case in range(cases)]
        crossed = [jnp.where(even, pltpu.roll(w, 7, 0), pltpu.roll(w, 1, 0)) for w in waves]
        for child in range(8):
            octant = child_ref[box, child]
            cosine, sine = turn_ref[octant, 0], turn_ref[octant, 1]
            for case in range(cases):
                made[arrival, case * 8 + child] = waves[case] * cosine + crossed[case] * sine
        pltpu.make_async_copy(made.at[arrival], out_ref.at[box], moved).start()
        return carry

    lax.fori_loop(0, boxes, one_box, 0, unroll=2)
    pltpu.make_async_copy(made, out_ref, moved).wait()


def whole(space):
    return pl.BlockSpec(memory_space=space)


def limit(mebibytes):
    return pltpu.CompilerParams(vmem_limit_bytes=mebibytes * 2**20)


def near(array):
    return pltpu.with_memory_space_constraint(array, pltpu.VMEM)


def far(array):
    return pltpu.with_memory_space_constraint(array, pltpu.HBM)


def pack(owner_slot, coefficients, sub_count):
    box_count = coefficients.shape[0]
    shape = (box_count, coefficients.size // (box_count * M), M)
    return pl.pallas_call(
        lambda *refs: pack_kernel(sub_count, *refs),
        out_shape=(pltpu.VMEM(shape, F32), jax.ShapeDtypeStruct((sub_count, box_count), jnp.int32)),
        in_specs=[whole(pl.ANY)] * 2,
        out_specs=(whole(pltpu.VMEM), whole(pltpu.VMEM)),
        scratch_shapes=[
            pltpu.SMEM((box_count,), jnp.int32),
            pltpu.VMEM(shape, F32),
            pltpu.SemaphoreType.DMA,
            pltpu.SemaphoreType.DMA((4,)),
        ],
        compiler_params=limit(16),
        name="pack",
    )(far(owner_slot), far(coefficients.reshape(shape)))


def stage(places, blk_count):
    high, rest = dft_halves()
    tables = [legendre_half(), high, rest, np.stack(shift_tables(blk_count), axis=2)]
    tables = [jnp.asarray(table) for table in tables]
    shapes = [table.shape for table in tables[:3]] + [tables[3].shape[1:]]
    return pl.pallas_call(
        stage_kernel,
        out_shape=[pltpu.VMEM(shape, table.dtype) for shape, table in zip(shapes, tables)],
        in_specs=[whole(pl.ANY)] * 5,
        out_specs=[whole(pltpu.VMEM)] * 4,
        scratch_shapes=[pltpu.SemaphoreType.DMA((4,))],
        compiler_params=limit(4),
        cost_estimate=pl.CostEstimate(flops=0, bytes_accessed=4 * 2**20, transcendentals=0),
        name="stage",
    )(*[far(table) for table in tables], places)


def transform(arrived, table, high, rest, blk_count):
    boxes = arrived.shape[0] // blk_count
    made = (blk_count, boxes, 8, K)
    return pl.pallas_call(
        lambda *refs: transform_kernel(blk_count, *refs),
        out_shape=jax.ShapeDtypeStruct(made, F32),
        in_specs=[whole(pltpu.VMEM)] * 4,
        out_specs=whole(pl.ANY),
        scratch_shapes=[
            pltpu.VMEM((2, 2 * J, 2 * M), F32),
            pltpu.VMEM(made, F32),
            pltpu.SemaphoreType.DMA,
        ],
        compiler_params=limit(16),
        name="transform",
    )(near(arrived), near(table), near(high), near(rest))


def shift(places, child_list, rows, turns):
    sub_count, boxes = places.shape
    cases = rows.shape[0] * sub_count // boxes
    shape = (boxes, cases * 8, 8, K)
    return pl.pallas_call(
        lambda *refs: shift_kernel(boxes, sub_count, *refs),
        out_shape=jax.ShapeDtypeStruct(shape, F32),
        in_specs=[whole(pltpu.SMEM)] * 2 + [whole(pltpu.VMEM)] * 2,
        out_specs=whole(pl.ANY),
        scratch_shapes=[pltpu.VMEM(shape, F32), pltpu.SemaphoreType.DMA],
        compiler_params=limit(16),
        name="shift",
    )(places, child_list, near(rows), near(turns))


def body(coefficients, owner_slot, child_list):
    box_count, cases = coefficients.shape[:2]
    blk_count = lax.axis_size("blk")

    outgoing, places = pack(owner_slot, coefficients, lax.axis_size("sub"))
    arrived = lax.all_to_all(outgoing.reshape(box_count * cases, 8, M), ("sub", "blk"), 0, 0, tiled=True)
    table, high, rest, turns = stage(places, blk_count)
    waves = transform(arrived, table, high, rest, blk_count)
    rows = lax.all_to_all(waves, "blk", 0, 0, tiled=True)
    places = lax.psum(places, "sub")
    children = shift(places, child_list, rows, turns)
    return children.reshape(box_count, cases, 8, J // blk_count, 2, K)


def solution(mesh):
    placed = (P("sub", None, None, "blk", None), P("sub"), P("sub", None))
    return jax.shard_map(
        body,
        mesh=mesh,
        in_specs=placed,
        out_specs=P("sub", None, None, "blk", None, None),
        check_vma=False,
    )
```

```python
import math

import jax
import jax.numpy as jnp
import ml_dtypes
import numpy as np
from jax import lax
from jax.experimental import pallas as pl
from jax.experimental.pallas import tpu as pltpu
from jax.sharding import PartitionSpec as P

L = 64
M = 128
J = 64
K = 128
HALF = J // 2
F32 = jnp.float32
BF16 = jnp.bfloat16


def legendre_half():
    order = np.abs(np.arange(M) - L).astype(np.float64)[None, :]
    polar = (np.pi * (np.arange(HALF) + 0.5) / J)[:, None]
    cosines, sines = np.cos(polar), np.sin(polar)
    lgamma = np.vectorize(math.lgamma)
    start = np.exp(
        0.5 * (np.log((2 * order + 1) / (4 * np.pi)) + lgamma(2 * order + 1) - order * np.log(4.0) - 2 * lgamma(order + 1))
        + order * np.log(sines)
    )
    following = np.sqrt(2 * order + 3) * cosines * start
    previous = before = np.zeros_like(start)
    factor_before = np.ones_like(order)
    rows = []
    for degree in range(L):
        factor = np.sqrt(np.maximum(4.0 * degree * degree - 1, 1) / np.maximum(degree * degree - order * order, 1))
        recur = factor * (cosines * previous - before / factor_before)
        value = np.where(degree < order, 0.0, np.where(degree == order, start, np.where(degree == order + 1, following, recur)))
        rows.append(value)
        previous, before, factor_before = value, previous, factor
    return np.stack(rows).astype(np.float32)


def dft_halves():
    turns = ((np.arange(M)[:, None] - L) * np.arange(K)[None, :]) % K
    angle = 2 * np.pi * turns / K
    cosine, sine = np.cos(angle), np.sin(angle)
    full = np.block([[cosine, sine], [-sine, cosine]])
    high = full.astype(ml_dtypes.bfloat16)
    rest = (full - high.astype(np.float64)).astype(ml_dtypes.bfloat16)
    return high, rest


def shift_tables(blk_count):
    polar = np.pi * (np.arange(J) + 0.5) / J
    azimuth = 2 * np.pi * np.arange(K) / K
    octant = np.arange(8)
    sign = [(2 * ((octant >> bit) & 1) - 1)[:, None, None] for bit in range(3)]
    phase = 5.5 * (
        sign[0] * (np.sin(polar)[:, None] * np.cos(azimuth))[None]
        + sign[1] * (np.sin(polar)[:, None] * np.sin(azimuth))[None]
        + sign[2] * (np.cos(polar)[:, None] * np.ones(K))[None]
    )
    cosine = np.stack([np.cos(phase), np.cos(phase)], axis=2)
    sine = np.stack([-np.sin(phase), np.sin(phase)], axis=2)
    width = J // blk_count

    def cut(table):
        table = table.reshape(8, blk_count, width * 2, K)
        return np.ascontiguousarray(table.transpose(1, 0, 2, 3)).astype(np.float32)

    return cut(cosine), cut(sine)


def pack_kernel(sub_count, slot_hbm, coef_hbm, out_ref, place_ref, slot_ref, held, slot_in, coef_in):
    box_count = coef_hbm.shape[0]
    per_peer = box_count // sub_count
    pieces = coef_in.shape[0]
    cut = box_count // pieces
    slots = pltpu.make_async_copy(slot_hbm, slot_ref, slot_in)
    slots.start()
    arriving = []
    for piece in range(pieces):
        part = pl.ds(piece * cut, cut)
        arriving.append(pltpu.make_async_copy(coef_hbm.at[part], held.at[part], coef_in.at[piece]))
    for copy in arriving:
        copy.start()
    row = lax.broadcasted_iota(jnp.int32, place_ref.shape, 0)
    lane = lax.broadcasted_iota(jnp.int32, place_ref.shape, 1)
    key = row * box_count + lane - lax.axis_index("sub") * per_peer
    place = jnp.zeros(place_ref.shape, jnp.int32)
    half = sub_count // 2
    cases = coef_hbm.shape[1] // 8
    counts = [jnp.int32(0), jnp.int32(0)]
    ranks = []
    slots.wait()
    for box in range(box_count):
        slot = slot_ref[box]
        peer = slot // box_count
        second = peer >= half
        shift_by = (peer % half) * 4
        word = jnp.where(second, counts[1], counts[0])
        rank = (word >> shift_by) & 7
        word = word + (jnp.int32(1) << shift_by)
        counts = [jnp.where(second, counts[0], word), jnp.where(second, word, counts[1])]
        place = jnp.where(key == peer * box_count + rank, slot % box_count, place)
        ranks.append((rank, peer))
    place_ref[...] = place
    for box in range(box_count):
        if box % cut == 0:
            arriving[box // cut].wait()
        rank, peer = ranks[box]
        for case in range(cases):
            out_ref[rank * cases + case, peer] = held[box, 8 * case : 8 * case + 8, :]


def stage_kernel(table_hbm, high_hbm, rest_hbm, turn_hbm, place_ref, table_ref, high_ref, rest_ref, turn_ref, moved):
    del place_ref
    pairs = [
        (table_hbm, table_ref),
        (high_hbm, high_ref),
        (rest_hbm, rest_ref),
        (turn_hbm.at[lax.axis_index("blk")], turn_ref),
    ]
    copies = [pltpu.make_async_copy(source, target, moved.at[at]) for at, (source, target) in enumerate(pairs)]
    for copy in copies:
        copy.start()
    for copy in copies:
        copy.wait()


def spread(value, order):
    return jnp.take_along_axis(value, order, axis=0)


def transform_kernel(blk_count, in_ref, table_ref, high_ref, rest_ref, place_ref, out_ref, cycles, made, moved):
    del place_ref
    boxes = in_ref.shape[1]
    degrees = L // blk_count
    group = 2
    vregs = HALF // 8
    lane = lax.broadcasted_iota(jnp.int32, (8, M), 1)
    mirror = jnp.where(lane % 2 == 0, 1.0, -1.0).astype(F32)

    def legendre(step, slot):
        sums = [[[None] * vregs for _ in range(2)] for _ in range(2 * group)]
        for degree in range(L):
            source, row = degree // degrees, degree % degrees
            table = [table_ref[degree, 8 * v : 8 * v + 8, :] for v in range(vregs)]
            for one in range(2 * group):
                box, part = step * group + one // 2, one % 2
                at = part * degrees + row
                value = in_ref[source, box, at : at + 1, :]
                wide = jnp.broadcast_to(value, (8, M))
                for v in range(vregs):
                    term = wide * table[v]
                    old = sums[one][degree % 2][v]
                    sums[one][degree % 2][v] = term if old is None else old + term
        for one in range(2 * group):
            box, part = one // 2, one % 2
            for v in range(vregs):
                even, odd = sums[one][0][v], sums[one][1][v]
                low, high = box * J + 8 * v, box * J + HALF + 8 * v
                cycles[slot, low : low + 8, part * M : part * M + M] = even + odd
                cycles[slot, high : high + 8, part * M : part * M + M] = (even - odd) * mirror

    width = J // blk_count
    sub_row = lax.broadcasted_iota(jnp.int32, (8, K), 0)
    real_row = sub_row % 2 == 0
    step_row = sub_row // 2

    def azimuths(step, slot):
        left = cycles[slot]
        left_high = left.astype(BF16)
        left_rest = (left - left_high.astype(F32)).astype(BF16)
        waves = jnp.dot(left_high, high_ref[...], preferred_element_type=F32)
        waves += jnp.dot(left_rest, high_ref[...], preferred_element_type=F32)
        waves += jnp.dot(left_high, rest_ref[...], preferred_element_type=F32)
        for one in range(group):
            for blk in range(blk_count):
                first = blk * width
                if first < HALF:
                    at, order = first // 8 * 8, first % 8 + step_row
                else:
                    low = J - 1 - first
                    at, order = HALF + low // 8 * 8, low % 8 - step_row
                start = one * J + at
                real = spread(waves[start : start + 8, :K], order)
                imag = spread(waves[start : start + 8, K:], order)
                made[step * group + one, blk] = jnp.where(real_row, real, imag)
        part = pl.ds(step * group, group)
        pltpu.make_async_copy(made.at[part], out_ref.at[part], moved).start()

    steps = boxes // group
    legendre(0, 0)
    for step in range(1, steps):
        azimuths(step - 1, (step - 1) % 2)
        legendre(step, step % 2)
    azimuths(steps - 1, (steps - 1) % 2)
    pltpu.make_async_copy(made, out_ref, moved).wait()


def shift_kernel(boxes, sub_count, place_ref, child_ref, in_ref, turn_ref, out_ref, made, moved):
    per_peer = boxes // sub_count
    cases = 4
    even = lax.broadcasted_iota(jnp.int32, (8, K), 0) % 2 == 0
    me = lax.axis_index("sub")

    def one_box(arrival, carry):
        box = place_ref[me, arrival]
        source = arrival // per_peer
        rank = arrival % per_peer
        waves = [in_ref[source, rank * cases + case] for case in range(cases)]
        crossed = [jnp.where(even, pltpu.roll(w, 7, 0), pltpu.roll(w, 1, 0)) for w in waves]
        for child in range(8):
            octant = child_ref[box, child]
            cosine, sine = turn_ref[octant, 0], turn_ref[octant, 1]
            for case in range(cases):
                made[arrival, case * 8 + child] = waves[case] * cosine + crossed[case] * sine
        pltpu.make_async_copy(made.at[arrival], out_ref.at[box], moved).start()
        return carry

    lax.fori_loop(0, boxes, one_box, 0, unroll=2)
    pltpu.make_async_copy(made, out_ref, moved).wait()


def whole(space):
    return pl.BlockSpec(memory_space=space)


def limit(mebibytes):
    return pltpu.CompilerParams(vmem_limit_bytes=mebibytes * 2**20)


def near(array):
    return pltpu.with_memory_space_constraint(array, pltpu.VMEM)


def far(array):
    return pltpu.with_memory_space_constraint(array, pltpu.HBM)


def pack(owner_slot, coefficients, sub_count):
    box_count = coefficients.shape[0]
    shape = (box_count, coefficients.size // (box_count * M), M)
    sent = (box_count // sub_count * coefficients.shape[1], sub_count, 8, M)
    return pl.pallas_call(
        lambda *refs: pack_kernel(sub_count, *refs),
        out_shape=(pltpu.VMEM(sent, F32), jax.ShapeDtypeStruct((sub_count, box_count), jnp.int32)),
        in_specs=[whole(pl.ANY)] * 2,
        out_specs=(whole(pltpu.VMEM), whole(pltpu.VMEM)),
        scratch_shapes=[
            pltpu.SMEM((box_count,), jnp.int32),
            pltpu.VMEM(shape, F32),
            pltpu.SemaphoreType.DMA,
            pltpu.SemaphoreType.DMA((4,)),
        ],
        compiler_params=limit(16),
        name="pack",
    )(far(owner_slot), far(coefficients.reshape(shape)))


def stage(places, blk_count):
    high, rest = dft_halves()
    tables = [legendre_half(), high, rest, np.stack(shift_tables(blk_count), axis=2)]
    tables = [jnp.asarray(table) for table in tables]
    shapes = [table.shape for table in tables[:3]] + [tables[3].shape[1:]]
    return pl.pallas_call(
        stage_kernel,
        out_shape=[pltpu.VMEM(shape, table.dtype) for shape, table in zip(shapes, tables)],
        in_specs=[whole(pl.ANY)] * 5,
        out_specs=[whole(pltpu.VMEM)] * 4,
        scratch_shapes=[pltpu.SemaphoreType.DMA((4,))],
        compiler_params=limit(4),
        cost_estimate=pl.CostEstimate(flops=0, bytes_accessed=4 * 2**20, transcendentals=0),
        name="stage",
    )(*[far(table) for table in tables], places)


def transform(arrived, table, high, rest, places):
    blk_count, boxes = arrived.shape[:2]
    made = (boxes, blk_count, 8, K)
    return pl.pallas_call(
        lambda *refs: transform_kernel(blk_count, *refs),
        out_shape=jax.ShapeDtypeStruct(made, F32),
        in_specs=[whole(pltpu.VMEM)] * 4 + [whole(pl.ANY)],
        out_specs=whole(pl.ANY),
        scratch_shapes=[
            pltpu.VMEM((2, 2 * J, 2 * M), F32),
            pltpu.VMEM(made, F32),
            pltpu.SemaphoreType.DMA,
        ],
        compiler_params=limit(16),
        name="transform",
    )(near(arrived), near(table), near(high), near(rest), places)


def shift(places, child_list, rows, turns):
    sub_count, boxes = places.shape
    cases = rows.shape[1] * sub_count // boxes
    shape = (boxes, cases * 8, 8, K)
    return pl.pallas_call(
        lambda *refs: shift_kernel(boxes, sub_count, *refs),
        out_shape=jax.ShapeDtypeStruct(shape, F32),
        in_specs=[whole(pltpu.SMEM)] * 2 + [whole(pltpu.VMEM)] * 2,
        out_specs=whole(pl.ANY),
        scratch_shapes=[pltpu.VMEM(shape, F32), pltpu.SemaphoreType.DMA],
        compiler_params=limit(16),
        name="shift",
    )(places, child_list, near(rows), near(turns))


def body(coefficients, owner_slot, child_list):
    box_count, cases = coefficients.shape[:2]
    blk_count = lax.axis_size("blk")

    outgoing, places = pack(owner_slot, coefficients, lax.axis_size("sub"))
    arrived = lax.all_to_all(outgoing, "blk", 0, 0, tiled=True)
    table, high, rest, turns = stage(places, blk_count)
    places = lax.psum(places, "sub")
    waves = transform(arrived, table, high, rest, places)
    rows = lax.all_to_all(waves.reshape(-1, 8, K), ("sub", "blk"), 0, 0, tiled=True).reshape(waves.shape)
    children = shift(places, child_list, rows, turns)
    return children.reshape(box_count, cases, 8, J // blk_count, 2, K)


def solution(mesh):
    placed = (P("sub", None, None, "blk", None), P("sub"), P("sub", None))
    return jax.shard_map(
        body,
        mesh=mesh,
        in_specs=placed,
        out_specs=P("sub", None, None, "blk", None, None),
        check_vma=False,
    )
```

```python
import math

import jax
import jax.numpy as jnp
import ml_dtypes
import numpy as np
from jax import lax
from jax.experimental import pallas as pl
from jax.experimental.pallas import tpu as pltpu
from jax.sharding import PartitionSpec as P

L = 64
M = 128
J = 64
K = 128
HALF = J // 2
F32 = jnp.float32
BF16 = jnp.bfloat16


def legendre_half():
    order = np.abs(np.arange(M) - L).astype(np.float64)[None, :]
    polar = (np.pi * (np.arange(HALF) + 0.5) / J)[:, None]
    cosines, sines = np.cos(polar), np.sin(polar)
    lgamma = np.vectorize(math.lgamma)
    start = np.exp(
        0.5 * (np.log((2 * order + 1) / (4 * np.pi)) + lgamma(2 * order + 1) - order * np.log(4.0) - 2 * lgamma(order + 1))
        + order * np.log(sines)
    )
    following = np.sqrt(2 * order + 3) * cosines * start
    previous = before = np.zeros_like(start)
    factor_before = np.ones_like(order)
    rows = []
    for degree in range(L):
        factor = np.sqrt(np.maximum(4.0 * degree * degree - 1, 1) / np.maximum(degree * degree - order * order, 1))
        recur = factor * (cosines * previous - before / factor_before)
        value = np.where(degree < order, 0.0, np.where(degree == order, start, np.where(degree == order + 1, following, recur)))
        rows.append(value)
        previous, before, factor_before = value, previous, factor
    return np.stack(rows).astype(np.float32)


def dft_halves():
    turns = ((np.arange(M)[:, None] - L) * np.arange(K)[None, :]) % K
    angle = 2 * np.pi * turns / K
    cosine, sine = np.cos(angle), np.sin(angle)
    full = np.block([[cosine, sine], [-sine, cosine]])
    high = full.astype(ml_dtypes.bfloat16)
    rest = (full - high.astype(np.float64)).astype(ml_dtypes.bfloat16)
    return high, rest


def shift_tables(blk_count):
    polar = np.pi * (np.arange(J) + 0.5) / J
    azimuth = 2 * np.pi * np.arange(K) / K
    octant = np.arange(8)
    sign = [(2 * ((octant >> bit) & 1) - 1)[:, None, None] for bit in range(3)]
    phase = 5.5 * (
        sign[0] * (np.sin(polar)[:, None] * np.cos(azimuth))[None]
        + sign[1] * (np.sin(polar)[:, None] * np.sin(azimuth))[None]
        + sign[2] * (np.cos(polar)[:, None] * np.ones(K))[None]
    )
    cosine = np.stack([np.cos(phase), np.cos(phase)], axis=2)
    sine = np.stack([-np.sin(phase), np.sin(phase)], axis=2)
    width = J // blk_count

    def cut(table):
        table = table.reshape(8, blk_count, width * 2, K)
        return np.ascontiguousarray(table.transpose(1, 0, 2, 3)).astype(np.float32)

    return cut(cosine), cut(sine)


def pack_kernel(sub_count, slot_hbm, coef_hbm, *refs):
    tables, refs = refs[:4], refs[4:]
    out_ref, place_ref, *staged = refs[:6]
    slot_ref, held, slot_in, coef_in, table_in = refs[6:]
    box_count = coef_hbm.shape[0]
    per_peer = box_count // sub_count
    pieces = coef_in.shape[0]
    cut = box_count // pieces
    slots = pltpu.make_async_copy(slot_hbm, slot_ref, slot_in)
    slots.start()
    arriving = []
    for piece in range(pieces):
        part = pl.ds(piece * cut, cut)
        arriving.append(pltpu.make_async_copy(coef_hbm.at[part], held.at[part], coef_in.at[piece]))
    for copy in arriving:
        copy.start()
    tables = tables[:3] + (tables[3].at[lax.axis_index("blk")],)
    staging = [pltpu.make_async_copy(a, b, table_in.at[at]) for at, (a, b) in enumerate(zip(tables, staged))]
    for copy in staging:
        copy.start()
    row = lax.broadcasted_iota(jnp.int32, place_ref.shape, 0)
    lane = lax.broadcasted_iota(jnp.int32, place_ref.shape, 1)
    key = row * place_ref.shape[1] + lane - lax.axis_index("sub") * per_peer
    place = jnp.zeros(place_ref.shape, jnp.int32)
    half = sub_count // 2
    cases = coef_hbm.shape[1] // 8
    counts = [jnp.int32(0), jnp.int32(0)]
    ranks = []
    slots.wait()
    for box in range(box_count):
        slot = slot_ref[box]
        peer = slot // box_count
        second = peer >= half
        shift_by = (peer % half) * 4
        word = jnp.where(second, counts[1], counts[0])
        rank = (word >> shift_by) & 7
        word = word + (jnp.int32(1) << shift_by)
        counts = [jnp.where(second, counts[0], word), jnp.where(second, word, counts[1])]
        place = jnp.where(key == peer * box_count + rank, slot % box_count, place)
        ranks.append((rank, peer))
    place_ref[...] = place
    for box in range(box_count):
        if box % cut == 0:
            arriving[box // cut].wait()
        rank, peer = ranks[box]
        for case in range(cases):
            out_ref[rank * cases + case, peer] = held[box, 8 * case : 8 * case + 8, :]
    for copy in staging:
        copy.wait()


def spread(value, order):
    return jnp.take_along_axis(value, order, axis=0)


def transform_kernel(blk_count, in_ref, table_ref, high_ref, rest_ref, place_ref, out_ref, cycles, made, moved):
    del place_ref
    boxes = in_ref.shape[1]
    degrees = L // blk_count
    group = 2
    vregs = HALF // 8
    lane = lax.broadcasted_iota(jnp.int32, (8, M), 1)
    mirror = jnp.where(lane % 2 == 0, 1.0, -1.0).astype(F32)

    def legendre(step, slot):
        sums = [[[None] * vregs for _ in range(2)] for _ in range(2 * group)]
        for degree in range(L):
            source, row = degree // degrees, degree % degrees
            table = [table_ref[degree, 8 * v : 8 * v + 8, :] for v in range(vregs)]
            for one in range(2 * group):
                box, part = step * group + one // 2, one % 2
                at = part * degrees + row
                value = in_ref[source, box, at : at + 1, :]
                wide = jnp.broadcast_to(value, (8, M))
                for v in range(vregs):
                    term = wide * table[v]
                    old = sums[one][degree % 2][v]
                    sums[one][degree % 2][v] = term if old is None else old + term
        for one in range(2 * group):
            box, part = one // 2, one % 2
            for v in range(vregs):
                even, odd = sums[one][0][v], sums[one][1][v]
                low, high = box * J + 8 * v, box * J + HALF + 8 * v
                cycles[slot, low : low + 8, part * M : part * M + M] = even + odd
                cycles[slot, high : high + 8, part * M : part * M + M] = (even - odd) * mirror

    width = J // blk_count
    sub_row = lax.broadcasted_iota(jnp.int32, (8, K), 0)
    real_row = sub_row % 2 == 0
    step_row = sub_row // 2

    def azimuths(step, slot):
        left = cycles[slot]
        left_high = left.astype(BF16)
        left_rest = (left - left_high.astype(F32)).astype(BF16)
        waves = jnp.dot(left_high, high_ref[...], preferred_element_type=F32)
        waves += jnp.dot(left_rest, high_ref[...], preferred_element_type=F32)
        waves += jnp.dot(left_high, rest_ref[...], preferred_element_type=F32)
        for one in range(group):
            for blk in range(blk_count):
                first = blk * width
                if first < HALF:
                    at, order = first // 8 * 8, first % 8 + step_row
                else:
                    low = J - 1 - first
                    at, order = HALF + low // 8 * 8, low % 8 - step_row
                start = one * J + at
                real = spread(waves[start : start + 8, :K], order)
                imag = spread(waves[start : start + 8, K:], order)
                made[step * group + one, blk] = jnp.where(real_row, real, imag)
        part = pl.ds(step * group, group)
        pltpu.make_async_copy(made.at[part], out_ref.at[part], moved).start()

    steps = boxes // group
    legendre(0, 0)
    for step in range(1, steps):
        azimuths(step - 1, (step - 1) % 2)
        legendre(step, step % 2)
    azimuths(steps - 1, (steps - 1) % 2)
    pltpu.make_async_copy(made, out_ref, moved).wait()


def shift_kernel(boxes, sub_count, place_ref, child_ref, in_ref, turn_ref, out_ref, made, moved):
    per_peer = boxes // sub_count
    cases = 4
    even = lax.broadcasted_iota(jnp.int32, (8, K), 0) % 2 == 0
    me = lax.axis_index("sub")

    def one_box(arrival, carry):
        at = me * boxes + arrival
        box = place_ref[at // 128, at % 128]
        source = arrival // per_peer
        rank = arrival % per_peer
        waves = [in_ref[source, rank * cases + case] for case in range(cases)]
        crossed = [jnp.where(even, pltpu.roll(w, 7, 0), pltpu.roll(w, 1, 0)) for w in waves]
        for child in range(8):
            octant = child_ref[box, child]
            cosine, sine = turn_ref[octant, 0], turn_ref[octant, 1]
            for case in range(cases):
                made[arrival, case * 8 + child] = waves[case] * cosine + crossed[case] * sine
        pltpu.make_async_copy(made.at[arrival], out_ref.at[box], moved).start()
        return carry

    lax.fori_loop(0, boxes, one_box, 0, unroll=2)
    pltpu.make_async_copy(made, out_ref, moved).wait()


def whole(space):
    return pl.BlockSpec(memory_space=space)


def limit(mebibytes):
    return pltpu.CompilerParams(vmem_limit_bytes=mebibytes * 2**20)


def near(array):
    return pltpu.with_memory_space_constraint(array, pltpu.VMEM)


def far(array):
    return pltpu.with_memory_space_constraint(array, pltpu.HBM)


def pack(owner_slot, coefficients, sub_count, blk_count):
    high, rest = dft_halves()
    tables = [legendre_half(), high, rest, np.stack(shift_tables(blk_count), axis=2)]
    tables = [jnp.asarray(table) for table in tables]
    shapes = [table.shape for table in tables[:3]] + [tables[3].shape[1:]]
    box_count = coefficients.shape[0]
    shape = (box_count, coefficients.size // (box_count * M), M)
    sent = (box_count // sub_count * coefficients.shape[1], sub_count, 8, M)
    return pl.pallas_call(
        lambda *refs: pack_kernel(sub_count, *refs),
        out_shape=(pltpu.VMEM(sent, F32), jax.ShapeDtypeStruct((sub_count * box_count // 128, 128), jnp.int32))
        + tuple(pltpu.VMEM(shape, table.dtype) for shape, table in zip(shapes, tables)),
        in_specs=[whole(pl.ANY)] * 6,
        out_specs=(whole(pltpu.VMEM),) * 6,
        scratch_shapes=[
            pltpu.SMEM((box_count,), jnp.int32),
            pltpu.VMEM(shape, F32),
            pltpu.SemaphoreType.DMA,
            pltpu.SemaphoreType.DMA((4,)),
            pltpu.SemaphoreType.DMA((4,)),
        ],
        compiler_params=limit(16),
        name="pack",
    )(far(owner_slot), far(coefficients.reshape(shape)), *[far(table) for table in tables])


def transform(arrived, table, high, rest, places):
    blk_count, boxes = arrived.shape[:2]
    made = (boxes, blk_count, 8, K)
    return pl.pallas_call(
        lambda *refs: transform_kernel(blk_count, *refs),
        out_shape=jax.ShapeDtypeStruct(made, F32),
        in_specs=[whole(pltpu.VMEM)] * 4 + [whole(pl.ANY)],
        out_specs=whole(pl.ANY),
        scratch_shapes=[
            pltpu.VMEM((2, 2 * J, 2 * M), F32),
            pltpu.VMEM(made, F32),
            pltpu.SemaphoreType.DMA,
        ],
        compiler_params=limit(16),
        name="transform",
    )(near(arrived), near(table), near(high), near(rest), places)


def shift(places, child_list, rows, turns):
    boxes, sub_count = child_list.shape[0], rows.shape[0]
    cases = rows.shape[1] * sub_count // boxes
    shape = (boxes, cases * 8, 8, K)
    return pl.pallas_call(
        lambda *refs: shift_kernel(boxes, sub_count, *refs),
        out_shape=jax.ShapeDtypeStruct(shape, F32),
        in_specs=[whole(pltpu.SMEM)] * 2 + [whole(pltpu.VMEM)] * 2,
        out_specs=whole(pl.ANY),
        scratch_shapes=[pltpu.VMEM(shape, F32), pltpu.SemaphoreType.DMA],
        compiler_params=limit(16),
        name="shift",
    )(places, child_list, near(rows), near(turns))


def body(coefficients, owner_slot, child_list):
    box_count, cases = coefficients.shape[:2]
    blk_count = lax.axis_size("blk")

    outgoing, places, table, high, rest, turns = pack(owner_slot, coefficients, lax.axis_size("sub"), blk_count)
    arrived = lax.all_to_all(outgoing, "blk", 0, 0, tiled=True)
    places = lax.psum(places, "sub")
    waves = transform(arrived, table, high, rest, places)
    rows = lax.all_to_all(waves.reshape(-1, 8, K), ("sub", "blk"), 0, 0, tiled=True).reshape(waves.shape)
    children = shift(places, child_list, rows, turns)
    return children.reshape(box_count, cases, 8, J // blk_count, 2, K)


def solution(mesh):
    placed = (P("sub", None, None, "blk", None), P("sub"), P("sub", None))
    return jax.shard_map(
        body,
        mesh=mesh,
        in_specs=placed,
        out_specs=P("sub", None, None, "blk", None, None),
        check_vma=False,
    )
```

```python
import math

import jax
import jax.numpy as jnp
import ml_dtypes
import numpy as np
from jax import lax
from jax.experimental import pallas as pl
from jax.experimental.pallas import tpu as pltpu
from jax.sharding import PartitionSpec as P

L = 64
M = 128
J = 64
K = 128
HALF = J // 2
F32 = jnp.float32
BF16 = jnp.bfloat16


def legendre_half():
    order = np.abs(np.arange(M) - L).astype(np.float64)[None, :]
    polar = (np.pi * (np.arange(HALF) + 0.5) / J)[:, None]
    cosines, sines = np.cos(polar), np.sin(polar)
    lgamma = np.vectorize(math.lgamma)
    start = np.exp(
        0.5 * (np.log((2 * order + 1) / (4 * np.pi)) + lgamma(2 * order + 1) - order * np.log(4.0) - 2 * lgamma(order + 1))
        + order * np.log(sines)
    )
    following = np.sqrt(2 * order + 3) * cosines * start
    previous = before = np.zeros_like(start)
    factor_before = np.ones_like(order)
    rows = []
    for degree in range(L):
        factor = np.sqrt(np.maximum(4.0 * degree * degree - 1, 1) / np.maximum(degree * degree - order * order, 1))
        recur = factor * (cosines * previous - before / factor_before)
        value = np.where(degree < order, 0.0, np.where(degree == order, start, np.where(degree == order + 1, following, recur)))
        rows.append(value)
        previous, before, factor_before = value, previous, factor
    return np.stack(rows).astype(np.float32)


def dft_halves():
    turns = ((np.arange(M)[:, None] - L) * np.arange(K)[None, :]) % K
    angle = 2 * np.pi * turns / K
    cosine, sine = np.cos(angle), np.sin(angle)
    full = np.block([[cosine, sine], [-sine, cosine]])
    high = full.astype(ml_dtypes.bfloat16)
    rest = (full - high.astype(np.float64)).astype(ml_dtypes.bfloat16)
    return high, rest


def shift_tables(blk_count):
    polar = np.pi * (np.arange(J) + 0.5) / J
    azimuth = 2 * np.pi * np.arange(K) / K
    octant = np.arange(8)
    sign = [(2 * ((octant >> bit) & 1) - 1)[:, None, None] for bit in range(3)]
    phase = 5.5 * (
        sign[0] * (np.sin(polar)[:, None] * np.cos(azimuth))[None]
        + sign[1] * (np.sin(polar)[:, None] * np.sin(azimuth))[None]
        + sign[2] * (np.cos(polar)[:, None] * np.ones(K))[None]
    )
    cosine = np.stack([np.cos(phase), np.cos(phase)], axis=2)
    sine = np.stack([-np.sin(phase), np.sin(phase)], axis=2)
    width = J // blk_count

    def cut(table):
        table = table.reshape(8, blk_count, width * 2, K)
        return np.ascontiguousarray(table.transpose(1, 0, 2, 3)).astype(np.float32)

    return cut(cosine), cut(sine)


def pack_kernel(sub_count, slot_hbm, coef_hbm, *refs):
    tables, refs = refs[:4], refs[4:]
    out_ref, place_ref, *staged = refs[:6]
    slot_ref, held, slot_in, coef_in, table_in = refs[6:]
    box_count = coef_hbm.shape[0]
    per_peer = box_count // sub_count
    box_bits = box_count.bit_length() - 1
    pieces = coef_in.shape[0]
    cut = box_count // pieces
    slots = pltpu.make_async_copy(slot_hbm, slot_ref, slot_in)
    slots.start()
    arriving = []
    for piece in range(pieces):
        part = pl.ds(piece * cut, cut)
        arriving.append(pltpu.make_async_copy(coef_hbm.at[part], held.at[part], coef_in.at[piece]))
    for copy in arriving:
        copy.start()
    tables = tables[:3] + (tables[3].at[lax.axis_index("blk")],)
    staging = [pltpu.make_async_copy(a, b, table_in.at[at]) for at, (a, b) in enumerate(zip(tables, staged))]
    for copy in staging:
        copy.start()
    row = lax.broadcasted_iota(jnp.int32, place_ref.shape, 0)
    lane = lax.broadcasted_iota(jnp.int32, place_ref.shape, 1)
    key = row * place_ref.shape[1] + lane - lax.axis_index("sub") * per_peer
    place = jnp.zeros(place_ref.shape, jnp.int32)
    half = sub_count // 2
    cases = coef_hbm.shape[1] // 8
    counts = [jnp.int32(0), jnp.int32(0)]
    ranks = []
    slots.wait()
    for box in range(box_count):
        slot = slot_ref[box]
        peer = slot >> box_bits
        second = peer >= half
        shift_by = (peer & (half - 1)) << 2
        word = jnp.where(second, counts[1], counts[0])
        rank = (word >> shift_by) & 7
        word = word + (jnp.int32(1) << shift_by)
        counts = [jnp.where(second, counts[0], word), jnp.where(second, word, counts[1])]
        place = jnp.where(key == (peer << box_bits) + rank, slot & (box_count - 1), place)
        ranks.append((rank, peer))
    place_ref[...] = place
    for box in range(box_count):
        if box % cut == 0:
            arriving[box // cut].wait()
        rank, peer = ranks[box]
        for case in range(cases):
            out_ref[rank * cases + case, peer] = held[box, 8 * case : 8 * case + 8, :]
    for copy in staging:
        copy.wait()


def spread(value, order):
    return jnp.take_along_axis(value, order, axis=0)


def transform_kernel(blk_count, in_ref, table_ref, high_ref, rest_ref, place_ref, out_ref, cycles, made, moved):
    del place_ref
    boxes = in_ref.shape[1]
    degrees = L // blk_count
    group = 2
    vregs = HALF // 8
    lane = lax.broadcasted_iota(jnp.int32, (8, M), 1)
    mirror = jnp.where(lane % 2 == 0, 1.0, -1.0).astype(F32)

    def legendre(step, slot):
        sums = [[[None] * vregs for _ in range(2)] for _ in range(2 * group)]
        for degree in range(L):
            source, row = degree // degrees, degree % degrees
            table = [table_ref[degree, 8 * v : 8 * v + 8, :] for v in range(vregs)]
            for one in range(2 * group):
                box, part = step * group + one // 2, one % 2
                at = part * degrees + row
                value = in_ref[source, box, at : at + 1, :]
                wide = jnp.broadcast_to(value, (8, M))
                for v in range(vregs):
                    term = wide * table[v]
                    old = sums[one][degree % 2][v]
                    sums[one][degree % 2][v] = term if old is None else old + term
        for one in range(2 * group):
            box, part = one // 2, one % 2
            for v in range(vregs):
                even, odd = sums[one][0][v], sums[one][1][v]
                low, high = box * J + 8 * v, box * J + HALF + 8 * v
                cycles[slot, low : low + 8, part * M : part * M + M] = even + odd
                cycles[slot, high : high + 8, part * M : part * M + M] = (even - odd) * mirror

    width = J // blk_count
    sub_row = lax.broadcasted_iota(jnp.int32, (8, K), 0)
    real_row = sub_row % 2 == 0
    step_row = sub_row // 2

    def azimuths(step, slot):
        left = cycles[slot]
        left_high = left.astype(BF16)
        left_rest = (left - left_high.astype(F32)).astype(BF16)
        waves = jnp.dot(left_high, high_ref[...], preferred_element_type=F32)
        waves += jnp.dot(left_rest, high_ref[...], preferred_element_type=F32)
        waves += jnp.dot(left_high, rest_ref[...], preferred_element_type=F32)
        for one in range(group):
            for blk in range(blk_count):
                first = blk * width
                if first < HALF:
                    at, order = first // 8 * 8, first % 8 + step_row
                else:
                    low = J - 1 - first
                    at, order = HALF + low // 8 * 8, low % 8 - step_row
                start = one * J + at
                real = spread(waves[start : start + 8, :K], order)
                imag = spread(waves[start : start + 8, K:], order)
                made[step * group + one, blk] = jnp.where(real_row, real, imag)
        part = pl.ds(step * group, group)
        pltpu.make_async_copy(made.at[part], out_ref.at[part], moved).start()

    steps = boxes // group
    legendre(0, 0)
    for step in range(1, steps):
        azimuths(step - 1, (step - 1) % 2)
        legendre(step, step % 2)
    azimuths(steps - 1, (steps - 1) % 2)
    pltpu.make_async_copy(made, out_ref, moved).wait()


def shift_kernel(boxes, sub_count, place_ref, child_ref, in_ref, turn_ref, out_ref, made, moved):
    per_peer = boxes // sub_count
    cases = 4
    even = lax.broadcasted_iota(jnp.int32, (8, K), 0) % 2 == 0
    me = lax.axis_index("sub")

    def one_box(arrival, carry):
        at = me * boxes + arrival
        box = place_ref[at >> 7, at & 127]
        source = arrival // per_peer
        rank = arrival % per_peer
        row, first = box >> 4, (box & 15) * 8
        waves = [in_ref[source, rank * cases + case] for case in range(cases)]
        crossed = [jnp.where(even, pltpu.roll(w, 7, 0), pltpu.roll(w, 1, 0)) for w in waves]
        for child in range(8):
            octant = child_ref[row, first + child]
            cosine, sine = turn_ref[octant, 0], turn_ref[octant, 1]
            for case in range(cases):
                made[arrival, case * 8 + child] = waves[case] * cosine + crossed[case] * sine
        pltpu.make_async_copy(made.at[arrival], out_ref.at[box], moved).start()
        return carry

    lax.fori_loop(0, boxes, one_box, 0, unroll=2)
    pltpu.make_async_copy(made, out_ref, moved).wait()


def whole(space):
    return pl.BlockSpec(memory_space=space)


def limit(mebibytes):
    return pltpu.CompilerParams(vmem_limit_bytes=mebibytes * 2**20)


def near(array):
    return pltpu.with_memory_space_constraint(array, pltpu.VMEM)


def far(array):
    return pltpu.with_memory_space_constraint(array, pltpu.HBM)


def pack(owner_slot, coefficients, sub_count, blk_count):
    high, rest = dft_halves()
    tables = [legendre_half(), high, rest, np.stack(shift_tables(blk_count), axis=2)]
    tables = [jnp.asarray(table) for table in tables]
    shapes = [table.shape for table in tables[:3]] + [tables[3].shape[1:]]
    box_count = coefficients.shape[0]
    shape = (box_count, coefficients.size // (box_count * M), M)
    sent = (box_count // sub_count * coefficients.shape[1], sub_count, 8, M)
    return pl.pallas_call(
        lambda *refs: pack_kernel(sub_count, *refs),
        out_shape=(pltpu.VMEM(sent, F32), jax.ShapeDtypeStruct((sub_count * box_count // 128, 128), jnp.int32))
        + tuple(pltpu.VMEM(shape, table.dtype) for shape, table in zip(shapes, tables)),
        in_specs=[whole(pl.ANY)] * 6,
        out_specs=(whole(pltpu.VMEM),) * 6,
        scratch_shapes=[
            pltpu.SMEM((box_count,), jnp.int32),
            pltpu.VMEM(shape, F32),
            pltpu.SemaphoreType.DMA,
            pltpu.SemaphoreType.DMA((4,)),
            pltpu.SemaphoreType.DMA((4,)),
        ],
        compiler_params=limit(16),
        name="pack",
    )(far(owner_slot), far(coefficients.reshape(shape)), *[far(table) for table in tables])


def transform(arrived, table, high, rest, places):
    blk_count, boxes = arrived.shape[:2]
    made = (boxes, blk_count, 8, K)
    return pl.pallas_call(
        lambda *refs: transform_kernel(blk_count, *refs),
        out_shape=jax.ShapeDtypeStruct(made, F32),
        in_specs=[whole(pltpu.VMEM)] * 4 + [whole(pl.ANY)],
        out_specs=whole(pl.ANY),
        scratch_shapes=[
            pltpu.VMEM((2, 2 * J, 2 * M), F32),
            pltpu.VMEM(made, F32),
            pltpu.SemaphoreType.DMA,
        ],
        compiler_params=limit(16),
        name="transform",
    )(near(arrived), near(table), near(high), near(rest), places)


def shift(places, child_list, rows, turns):
    boxes, sub_count = child_list.shape[0], rows.shape[0]
    child_list = child_list.reshape(-1, 128)
    cases = rows.shape[1] * sub_count // boxes
    shape = (boxes, cases * 8, 8, K)
    return pl.pallas_call(
        lambda *refs: shift_kernel(boxes, sub_count, *refs),
        out_shape=jax.ShapeDtypeStruct(shape, F32),
        in_specs=[whole(pltpu.SMEM)] * 2 + [whole(pltpu.VMEM)] * 2,
        out_specs=whole(pl.ANY),
        scratch_shapes=[pltpu.VMEM(shape, F32), pltpu.SemaphoreType.DMA],
        compiler_params=limit(16),
        name="shift",
    )(places, child_list, near(rows), near(turns))


def body(coefficients, owner_slot, child_list):
    box_count, cases = coefficients.shape[:2]
    blk_count = lax.axis_size("blk")

    outgoing, places, table, high, rest, turns = pack(owner_slot, coefficients, lax.axis_size("sub"), blk_count)
    arrived = lax.all_to_all(outgoing, "blk", 0, 0, tiled=True)
    places = lax.psum(places, "sub")
    waves = transform(arrived, table, high, rest, places)
    rows = lax.all_to_all(waves.reshape(-1, 8, K), ("sub", "blk"), 0, 0, tiled=True).reshape(waves.shape)
    children = shift(places, child_list, rows, turns)
    return children.reshape(box_count, cases, 8, J // blk_count, 2, K)


def solution(mesh):
    placed = (P("sub", None, None, "blk", None), P("sub"), P("sub", None))
    return jax.shard_map(
        body,
        mesh=mesh,
        in_specs=placed,
        out_specs=P("sub", None, None, "blk", None, None),
        check_vma=False,
    )
```

```python
import math

import jax
import jax.numpy as jnp
import ml_dtypes
import numpy as np
from jax import lax
from jax.experimental import pallas as pl
from jax.experimental.pallas import tpu as pltpu
from jax.sharding import PartitionSpec as P

L = 64
M = 128
J = 64
K = 128
HALF = J // 2
F32 = jnp.float32
BF16 = jnp.bfloat16


def legendre_half():
    order = np.abs(np.arange(M) - L).astype(np.float64)[None, :]
    polar = (np.pi * (np.arange(HALF) + 0.5) / J)[:, None]
    cosines, sines = np.cos(polar), np.sin(polar)
    lgamma = np.vectorize(math.lgamma)
    start = np.exp(
        0.5 * (np.log((2 * order + 1) / (4 * np.pi)) + lgamma(2 * order + 1) - order * np.log(4.0) - 2 * lgamma(order + 1))
        + order * np.log(sines)
    )
    following = np.sqrt(2 * order + 3) * cosines * start
    previous = before = np.zeros_like(start)
    factor_before = np.ones_like(order)
    rows = []
    for degree in range(L):
        factor = np.sqrt(np.maximum(4.0 * degree * degree - 1, 1) / np.maximum(degree * degree - order * order, 1))
        recur = factor * (cosines * previous - before / factor_before)
        value = np.where(degree < order, 0.0, np.where(degree == order, start, np.where(degree == order + 1, following, recur)))
        rows.append(value)
        previous, before, factor_before = value, previous, factor
    return np.stack(rows).astype(np.float32)


def dft_halves():
    turns = ((np.arange(M)[:, None] - L) * np.arange(K)[None, :]) % K
    angle = 2 * np.pi * turns / K
    cosine, sine = np.cos(angle), np.sin(angle)
    full = np.block([[cosine, sine], [-sine, cosine]])
    high = full.astype(ml_dtypes.bfloat16)
    rest = (full - high.astype(np.float64)).astype(ml_dtypes.bfloat16)
    return high, rest


def shift_tables(blk_count):
    polar = np.pi * (np.arange(J) + 0.5) / J
    azimuth = 2 * np.pi * np.arange(K) / K
    octant = np.arange(8)
    sign = [(2 * ((octant >> bit) & 1) - 1)[:, None, None] for bit in range(3)]
    phase = 5.5 * (
        sign[0] * (np.sin(polar)[:, None] * np.cos(azimuth))[None]
        + sign[1] * (np.sin(polar)[:, None] * np.sin(azimuth))[None]
        + sign[2] * (np.cos(polar)[:, None] * np.ones(K))[None]
    )
    cosine = np.stack([np.cos(phase), np.cos(phase)], axis=2)
    sine = np.stack([-np.sin(phase), np.sin(phase)], axis=2)
    width = J // blk_count

    def cut(table):
        table = table.reshape(8, blk_count, width * 2, K)
        return np.ascontiguousarray(table.transpose(1, 0, 2, 3)).astype(np.float32)

    return cut(cosine), cut(sine)


def pack_kernel(sub_count, slot_hbm, coef_hbm, *refs):
    tables, refs = refs[:4], refs[4:]
    out_ref, place_ref, *staged = refs[:6]
    slot_ref, held, slot_in, coef_in, table_in = refs[6:]
    box_count = coef_hbm.shape[0]
    per_peer = box_count // sub_count
    box_bits = box_count.bit_length() - 1
    pieces = coef_in.shape[0]
    cut = box_count // pieces
    slots = pltpu.make_async_copy(slot_hbm, slot_ref, slot_in)
    slots.start()
    arriving = []
    for piece in range(pieces):
        part = pl.ds(piece * cut, cut)
        arriving.append(pltpu.make_async_copy(coef_hbm.at[part], held.at[part], coef_in.at[piece]))
    for copy in arriving:
        copy.start()
    tables = tables[:3] + (tables[3].at[lax.axis_index("blk")],)
    staging = [pltpu.make_async_copy(a, b, table_in.at[at]) for at, (a, b) in enumerate(zip(tables, staged))]
    for copy in staging:
        copy.start()
    row = lax.broadcasted_iota(jnp.int32, place_ref.shape, 0)
    lane = lax.broadcasted_iota(jnp.int32, place_ref.shape, 1)
    key = row * place_ref.shape[1] + lane - lax.axis_index("sub") * per_peer
    place = jnp.zeros(place_ref.shape, jnp.int32)
    half = sub_count // 2
    cases = coef_hbm.shape[1] // 8
    counts = [jnp.int32(0), jnp.int32(0)]
    ranks = []
    slots.wait()
    for box in range(box_count):
        slot = slot_ref[box]
        peer = slot >> box_bits
        second = peer >= half
        shift_by = (peer & (half - 1)) << 2
        word = jnp.where(second, counts[1], counts[0])
        rank = (word >> shift_by) & 7
        word = word + (jnp.int32(1) << shift_by)
        counts = [jnp.where(second, counts[0], word), jnp.where(second, word, counts[1])]
        place = jnp.where(key == (peer << box_bits) + rank, slot & (box_count - 1), place)
        ranks.append((rank, peer))
    place_ref[...] = place
    for box in range(box_count):
        if box % cut == 0:
            arriving[box // cut].wait()
        rank, peer = ranks[box]
        for case in range(cases):
            out_ref[rank * cases + case, peer] = held[box, 8 * case : 8 * case + 8, :]
    for copy in staging:
        copy.wait()


def spread(value, order):
    return jnp.take_along_axis(value, order, axis=0)


def transform_kernel(blk_count, in_ref, table_ref, high_ref, rest_ref, place_ref, out_ref, cycles, made, moved):
    del place_ref
    boxes = in_ref.shape[1]
    degrees = L // blk_count
    vregs = HALF // 8
    lane = lax.broadcasted_iota(jnp.int32, (8, M), 1)
    mirror = jnp.where(lane % 2 == 0, 1.0, -1.0).astype(F32)

    def legendre(start_box, group, slot):
        sums = [[[None] * vregs for _ in range(2)] for _ in range(2 * group)]
        for degree in range(L):
            source, row = degree // degrees, degree % degrees
            table = [table_ref[degree, 8 * v : 8 * v + 8, :] for v in range(vregs)]
            for one in range(2 * group):
                box, part = start_box + one // 2, one % 2
                at = part * degrees + row
                value = in_ref[source, box, at : at + 1, :]
                wide = jnp.broadcast_to(value, (8, M))
                for v in range(vregs):
                    term = wide * table[v]
                    old = sums[one][degree % 2][v]
                    sums[one][degree % 2][v] = term if old is None else old + term
        for one in range(2 * group):
            box, part = one // 2, one % 2
            for v in range(vregs):
                even, odd = sums[one][0][v], sums[one][1][v]
                low, high = box * J + 8 * v, box * J + HALF + 8 * v
                cycles[slot, low : low + 8, part * M : part * M + M] = even + odd
                cycles[slot, high : high + 8, part * M : part * M + M] = (even - odd) * mirror

    width = J // blk_count
    sub_row = lax.broadcasted_iota(jnp.int32, (8, K), 0)
    real_row = sub_row % 2 == 0
    step_row = sub_row // 2

    def azimuths(start_box, group, slot):
        left = cycles[slot, : group * J]
        left_high = left.astype(BF16)
        left_rest = (left - left_high.astype(F32)).astype(BF16)
        waves = jnp.dot(left_high, high_ref[...], preferred_element_type=F32)
        waves += jnp.dot(left_rest, high_ref[...], preferred_element_type=F32)
        waves += jnp.dot(left_high, rest_ref[...], preferred_element_type=F32)
        for one in range(group):
            for blk in range(blk_count):
                first = blk * width
                if first < HALF:
                    at, order = first // 8 * 8, first % 8 + step_row
                else:
                    low = J - 1 - first
                    at, order = HALF + low // 8 * 8, low % 8 - step_row
                start = one * J + at
                real = spread(waves[start : start + 8, :K], order)
                imag = spread(waves[start : start + 8, K:], order)
                made[start_box + one, blk] = jnp.where(real_row, real, imag)
        part = pl.ds(start_box, group)
        pltpu.make_async_copy(made.at[part], out_ref.at[part], moved).start()

    sizes = [1] * boxes
    starts = [sum(sizes[:step]) for step in range(len(sizes))]
    legendre(starts[0], sizes[0], 0)
    for step in range(1, len(sizes)):
        azimuths(starts[step - 1], sizes[step - 1], (step - 1) % 2)
        legendre(starts[step], sizes[step], step % 2)
    azimuths(starts[-1], sizes[-1], (len(sizes) - 1) % 2)
    pltpu.make_async_copy(made, out_ref, moved).wait()


def shift_kernel(boxes, sub_count, place_ref, child_ref, in_ref, turn_ref, out_ref, made, moved):
    per_peer = boxes // sub_count
    cases = 4
    even = lax.broadcasted_iota(jnp.int32, (8, K), 0) % 2 == 0
    me = lax.axis_index("sub")

    def one_box(arrival, carry):
        at = me * boxes + arrival
        box = place_ref[at >> 7, at & 127]
        source = arrival // per_peer
        rank = arrival % per_peer
        row, first = box >> 4, (box & 15) * 8
        waves = [in_ref[source, rank * cases + case] for case in range(cases)]
        crossed = [jnp.where(even, pltpu.roll(w, 7, 0), pltpu.roll(w, 1, 0)) for w in waves]
        for child in range(8):
            octant = child_ref[row, first + child]
            cosine, sine = turn_ref[octant, 0], turn_ref[octant, 1]
            for case in range(cases):
                made[arrival, case * 8 + child] = waves[case] * cosine + crossed[case] * sine
        pltpu.make_async_copy(made.at[arrival], out_ref.at[box], moved).start()
        return carry

    lax.fori_loop(0, boxes, one_box, 0, unroll=2)
    pltpu.make_async_copy(made, out_ref, moved).wait()


def whole(space):
    return pl.BlockSpec(memory_space=space)


def limit(mebibytes):
    return pltpu.CompilerParams(vmem_limit_bytes=mebibytes * 2**20)


def near(array):
    return pltpu.with_memory_space_constraint(array, pltpu.VMEM)


def far(array):
    return pltpu.with_memory_space_constraint(array, pltpu.HBM)


def pack(owner_slot, coefficients, sub_count, blk_count):
    high, rest = dft_halves()
    tables = [legendre_half(), high, rest, np.stack(shift_tables(blk_count), axis=2)]
    tables = [jnp.asarray(table) for table in tables]
    shapes = [table.shape for table in tables[:3]] + [tables[3].shape[1:]]
    box_count = coefficients.shape[0]
    shape = (box_count, coefficients.size // (box_count * M), M)
    sent = (box_count // sub_count * coefficients.shape[1], sub_count, 8, M)
    return pl.pallas_call(
        lambda *refs: pack_kernel(sub_count, *refs),
        out_shape=(pltpu.VMEM(sent, F32), jax.ShapeDtypeStruct((sub_count * box_count // 128, 128), jnp.int32))
        + tuple(pltpu.VMEM(shape, table.dtype) for shape, table in zip(shapes, tables)),
        in_specs=[whole(pl.ANY)] * 6,
        out_specs=(whole(pltpu.VMEM),) * 6,
        scratch_shapes=[
            pltpu.SMEM((box_count,), jnp.int32),
            pltpu.VMEM(shape, F32),
            pltpu.SemaphoreType.DMA,
            pltpu.SemaphoreType.DMA((4,)),
            pltpu.SemaphoreType.DMA((4,)),
        ],
        compiler_params=limit(16),
        name="pack",
    )(far(owner_slot), far(coefficients.reshape(shape)), *[far(table) for table in tables])


def transform(arrived, table, high, rest, places):
    blk_count, boxes = arrived.shape[:2]
    made = (boxes, blk_count, 8, K)
    return pl.pallas_call(
        lambda *refs: transform_kernel(blk_count, *refs),
        out_shape=jax.ShapeDtypeStruct(made, F32),
        in_specs=[whole(pltpu.VMEM)] * 4 + [whole(pl.ANY)],
        out_specs=whole(pl.ANY),
        scratch_shapes=[
            pltpu.VMEM((2, 2 * J, 2 * M), F32),
            pltpu.VMEM(made, F32),
            pltpu.SemaphoreType.DMA,
        ],
        compiler_params=limit(16),
        name="transform",
    )(near(arrived), near(table), near(high), near(rest), places)


def shift(places, child_list, rows, turns):
    boxes, sub_count = child_list.shape[0], rows.shape[0]
    child_list = child_list.reshape(-1, 128)
    cases = rows.shape[1] * sub_count // boxes
    shape = (boxes, cases * 8, 8, K)
    return pl.pallas_call(
        lambda *refs: shift_kernel(boxes, sub_count, *refs),
        out_shape=jax.ShapeDtypeStruct(shape, F32),
        in_specs=[whole(pltpu.SMEM)] * 2 + [whole(pltpu.VMEM)] * 2,
        out_specs=whole(pl.ANY),
        scratch_shapes=[pltpu.VMEM(shape, F32), pltpu.SemaphoreType.DMA],
        compiler_params=limit(16),
        name="shift",
    )(places, child_list, near(rows), near(turns))


def body(coefficients, owner_slot, child_list):
    box_count, cases = coefficients.shape[:2]
    blk_count = lax.axis_size("blk")

    outgoing, places, table, high, rest, turns = pack(owner_slot, coefficients, lax.axis_size("sub"), blk_count)
    arrived = lax.all_to_all(outgoing, "blk", 0, 0, tiled=True)
    places = lax.psum(places, "sub")
    waves = transform(arrived, table, high, rest, places)
    rows = lax.all_to_all(waves.reshape(-1, 8, K), ("sub", "blk"), 0, 0, tiled=True).reshape(waves.shape)
    children = shift(places, child_list, rows, turns)
    return children.reshape(box_count, cases, 8, J // blk_count, 2, K)


def solution(mesh):
    placed = (P("sub", None, None, "blk", None), P("sub"), P("sub", None))
    return jax.shard_map(
        body,
        mesh=mesh,
        in_specs=placed,
        out_specs=P("sub", None, None, "blk", None, None),
        check_vma=False,
    )
```
